256 devices in a mesh: seq: 32 (over x, y, core), tp: 8 (over z).
Axes of the slice: x: 4, y: 4, z: 8, core: 2. Of those that a mesh axis runs over, the one named last changes fastest.
Arguments:
- text_embed: bfloat16 [16384, 4096], P('seq', 'tp'), may hold values from -16 to 16
- latents: bfloat16 [32, 256, 64], P('seq'), may hold values from -6 to 6
- noise: bfloat16 [32, 256, 64], P('seq'), may hold values from -6 to 6
- timesteps: int32 [32], P('seq'), may hold values from 0 to 999
- image_block: int32 [32], replicated, may hold values from 0 to 63, as said below
- doc_ids: int32 [16384], replicated, may hold values from 0 to 3, never falling along the last dimension, each value on 1 to 14336 neighbouring positions
- norm_gain: float32 [4096], replicated, may hold values from 0.1 to 1.9
- w_patch: bfloat16 [64, 4096], P(None, 'tp'), may hold values from -0.75 to 0.75
- w_time: bfloat16 [256, 4096], P(None, 'tp'), may hold values from -0.375 to 0.375
- w_qkv: bfloat16 [4096, 3, 2048], P(None, None, 'tp'), may hold values from -3 to 3
- w_out: bfloat16 [2048, 4096], P('tp'), may hold values from -0.125 to 0.125
- w_dec: bfloat16 [4096, 64], P('tp'), may hold values from -0.09375 to 0.09375
Outputs:
- hidden_out: bfloat16 [16384, 4096], P('seq', 'tp')
- predicted: float32 [16384, 64], P('seq')
- patch_error: float32 [16384], P('seq')
The draws below stay inside these ranges and needn't reach their ends.
Inputs may be any that keep to these rules, and one draw needn't show every extreme that they name: `image_block`: the blocks of different images are different.
All inputs are finite; a program needn't handle non-finite values.
Results may differ from the reference program's by a relative error of at most 0.024.
Values may be sent and summed in bfloat16 or wider, within the bound.
No kernel may reach another device: no remote copies, remote signals or barrier semaphores. Data moves between devices by JAX's collectives and lax.ppermute only.
A program may use at most 128 MiB of HBM per device.

```python
import math
import jax
import jax.numpy as jnp
import numpy as np
from jax import lax

D = 4096
HEADS = 16
HD = 128
PV = 64
PATCHES = 256
TFREQ = 128
TSTEPS = 1000
DOCS = 4
S = 16384
IMAGES = 32
N_TP = 8


def sink_parts(key):
    direction_key = jax.random.fold_in(key, 101)
    pattern_key = jax.random.fold_in(key, 102)
    choice_key = jax.random.fold_in(key, 103)
    sink_direction = jnp.clip(jax.random.normal(direction_key, (D,), jnp.float32), -3.0, 3.0)
    head_pattern = jnp.clip(jax.random.normal(pattern_key, (HD,), jnp.float32), -3.0, 3.0)
    chosen_head = jax.random.randint(choice_key, (), 0, HEADS)
    return (sink_direction, head_pattern, chosen_head)


def draw_text_embed(key, part):
    sink_direction, head_pattern, chosen_head = sink_parts(key)
    key = jax.random.fold_in(key, 11)
    rows_key = jax.random.fold_in(key, 1)
    offset_key = jax.random.fold_in(key, 2)
    amplitude_key = jax.random.fold_in(key, 3)
    base_rows = jnp.clip(jax.random.normal(rows_key, (S, D), jnp.float32), -6.0, 6.0)
    group_rows = math.gcd(S, 128)
    group_count = S // group_rows
    offsets = jax.random.randint(offset_key, (group_count,), 0, group_rows - 2)
    amplitude = jnp.exp(jax.random.uniform(amplitude_key, (group_count,), jnp.float32, 0.0, math.log(3.0)))
    inside = jnp.arange(group_rows, dtype=jnp.int32)[None, :] - offsets[:, None]
    run_mask = (inside >= 0) & (inside < 3)
    row_amplitude = jnp.where(run_mask, amplitude[:, None], 0.0).reshape(S)
    return (base_rows + row_amplitude[:, None] * sink_direction[None, :]).astype(jnp.bfloat16)


def draw_w_qkv(key, part):
    sink_direction, head_pattern, chosen_head = sink_parts(key)
    key = jax.random.fold_in(key, 13)
    weights = jnp.clip(jax.random.normal(key, (D, 3, HEADS, HD), jnp.float32), -6.0, 6.0) * (math.sqrt(3.0) / math.sqrt(D))
    strength = 5.5
    head_mask = (jnp.arange(HEADS, dtype=jnp.int32) == chosen_head).astype(jnp.float32)
    slot_mask = jnp.array([1.0, 1.0, 0.0], dtype=jnp.float32)
    aligned = strength / D * sink_direction[:, None, None, None] * slot_mask[None, :, None, None] * head_mask[None, None, :, None] * head_pattern[None, None, None, :]
    return (weights + aligned).reshape(D, 3, HEADS * HD).astype(jnp.bfloat16)


def draw_image_block(key, part):
    key = jax.random.fold_in(key, 7)
    first_key = jax.random.fold_in(key, 1)
    second_key = jax.random.fold_in(key, 2)
    n_blocks = S // PATCHES
    inner = jax.random.permutation(first_key, n_blocks - 2) + 1
    chosen = jnp.concatenate([jnp.array([0, n_blocks - 1], dtype=jnp.int32), inner[:IMAGES - 2].astype(jnp.int32)])
    return jax.random.permutation(second_key, chosen).astype(jnp.int32)


def touch_ends(values, own_key, least, top_value):
    longest = values.shape.index(max(values.shape))
    spots = []
    for shift in (0, 1):
        where = [jax.random.randint(jax.random.fold_in(own_key, axis), (), 0, length) for axis, length in enumerate(values.shape)]
        where[longest] = (where[longest] + shift) % values.shape[longest]
        spots.append(tuple(where))
    return values.at[spots[0]].set(least).at[spots[1]].set(top_value)


def levels(own_key, shape, shards, low, high):
    gain = 1.0
    for axis_at, blocks in shards:
        draws = jax.random.uniform(jax.random.fold_in(jax.random.fold_in(own_key, 6), axis_at), (blocks,), jnp.float32, low / len(shards), high / len(shards))
        gain = gain * jnp.repeat(jnp.exp(draws), shape[axis_at] // blocks).reshape((-1,) + (1,) * (len(shape) - 1 - axis_at))
    return gain


def split_up(count, total, most, slope):
    portions = [(1 << 20) // math.isqrt(grade ** slope) + 1 for grade in range(2, count + 1)]
    rest, given = total - most - (count - 1), [1] * (count - 1)
    while rest > 0:
        candidates = [i for i in range(count - 1) if given[i] < most]
        pool, budget = sum([portions[i] for i in candidates]), rest
        for i in candidates:
            extra = min(most - given[i], max(1, budget * portions[i] // pool), rest)
            given[i] = given[i] + extra
            rest = rest - extra
    return np.array([most] + given)


def uneven(key, number_of, total, limit, lean):
    if number_of == 2:
        one = jax.random.randint(key, (), max(1, total - limit), min(limit, total - 1) + 1)
        return jnp.stack([one, total - one])
    tallies = jnp.asarray(split_up(number_of, total, limit, lean), jnp.int32)
    twos = (number_of - 1) // 2
    giver, taker = tallies[1:1 + 2 * twos:2], tallies[2:2 + 2 * twos:2]
    margin = jnp.minimum(giver - 1, limit - taker)
    moved = jax.random.randint(jax.random.fold_in(key, 1), (twos,), 0, 1 << 20) % (margin + 1)
    tallies = tallies.at[1:1 + 2 * twos:2].set(giver - moved).at[2:2 + 2 * twos:2].set(taker + moved)
    return tallies[jax.random.permutation(jax.random.fold_in(key, 2), number_of)]


def normal_values(key, dims, deviation, reach, pieces=(), held_as=jnp.bfloat16):
    gain = levels(key, dims, pieces, -0.22, 0.18) if pieces else 1.0
    values = jax.random.normal(key, dims, jnp.float32) * deviation * gain
    return jnp.minimum(jnp.maximum(values, -reach), reach).astype(held_as)


def setup_inputs(seed: int = 0) -> dict:
    arg_keys = jax.random.split(jax.random.key(seed), 13)
    return {
        "text_embed": draw_text_embed(jax.random.fold_in(arg_keys[12], 71), 0),
        "latents": normal_values(arg_keys[1], (IMAGES, PATCHES, PV), 1.0, 6.0, ((0, 32),)),
        "noise": normal_values(arg_keys[2], (IMAGES, PATCHES, PV), 1.0, 6.0, ((0, 32),)),
        "timesteps": touch_ends(jax.random.randint(arg_keys[3], (IMAGES,), 0, TSTEPS), jax.random.fold_in(arg_keys[3], 1), 0, TSTEPS - 1).astype(jnp.int32),
        "image_block": draw_image_block(jax.random.fold_in(arg_keys[12], 71), 0),
        "doc_ids": jnp.searchsorted(jnp.cumsum(uneven(arg_keys[5], DOCS, S, S - S // 8, 2)), jnp.arange(S), side="right").astype(jnp.int32),
        "norm_gain": jnp.clip(1.0 + 0.18 * jax.random.normal(arg_keys[6], (D,), jnp.float32), 0.1, 1.9),
        "w_patch": normal_values(arg_keys[7], (PV, D), PV ** -0.5, 0.75, ((1, 8),)),
        "w_time": normal_values(arg_keys[8], (2 * TFREQ, D), (2 * TFREQ) ** -0.5, 0.375, ((1, 8),)),
        "w_qkv": draw_w_qkv(jax.random.fold_in(arg_keys[12], 71), 0),
        "w_out": normal_values(arg_keys[10], (HEADS * HD, D), (HEADS * HD) ** -0.5, 0.125, ((0, 8),)),
        "w_dec": normal_values(arg_keys[11], (D, PV), D ** -0.5, 0.09375, ((0, 8),)),
    }


epsilon = 1e-05
masked_score = -1e+30

def noisy_patches(latents, noise, timesteps):
    step_values = timesteps.astype(jnp.float32)
    signal_level = jnp.cos((step_values / TSTEPS + 0.008) / 1.008 * (math.pi / 2)) ** 2
    noised = (jnp.sqrt(signal_level)[:, None, None] * latents.astype(jnp.float32) + jnp.sqrt(1.0 - signal_level)[:, None, None] * noise.astype(jnp.float32)).astype(jnp.bfloat16)
    frequencies = jnp.exp(-math.log(10000.0) * jnp.arange(TFREQ, dtype=jnp.float32) / TFREQ)
    angles = step_values[:, None] * frequencies[None, :]
    time_feats = jnp.concatenate([jnp.cos(angles), jnp.sin(angles)], axis=1).astype(jnp.bfloat16)
    return (noised, time_feats)

def reference(text_embed, latents, noise, timesteps, image_block, doc_ids, norm_gain, w_patch, w_time, w_qkv, w_out, w_dec):
    noised, time_feats = noisy_patches(latents, noise, timesteps)
    patch_part = jnp.einsum('ipc,cd->ipd', noised.astype(jnp.float32), w_patch.astype(jnp.float32))
    time_part = jnp.dot(time_feats, w_time, preferred_element_type=jnp.float32)
    embedded = (patch_part + time_part[:, None, :]).astype(jnp.bfloat16)
    n_blocks = S // PATCHES
    residual = text_embed.reshape(n_blocks, PATCHES, D).at[image_block].set(embedded).reshape(S, D)
    wide = residual.astype(jnp.float32)
    inverse = lax.rsqrt(lax.optimization_barrier(jnp.mean(wide * wide, axis=1, keepdims=True)) + epsilon)
    normed = (wide * inverse * norm_gain[None, :]).astype(jnp.bfloat16)
    projected = jnp.dot(normed, w_qkv.reshape(D, 3 * HEADS * HD), preferred_element_type=jnp.float32)
    projected = projected.astype(jnp.bfloat16).reshape(S, 3, HEADS, HD)
    queries = projected[:, 0]
    key_rows = projected[:, 1].astype(jnp.float32)
    value_rows = projected[:, 2].astype(jnp.float32)
    image_flags = jnp.zeros((n_blocks,), jnp.int32).at[image_block].set(1)
    positions = jnp.arange(S, dtype=jnp.int32)
    blocks = positions // PATCHES
    block_len = math.gcd(S, 512)

    def query_block(first_query):
        query_pos = first_query + jnp.arange(block_len, dtype=jnp.int32)
        query_rows = lax.dynamic_slice_in_dim(queries, first_query, block_len, 0).astype(jnp.float32)
        query_docs = lax.dynamic_slice_in_dim(doc_ids, first_query, block_len, 0)
        query_blocks = query_pos // PATCHES
        query_image = image_flags[query_blocks] == 1
        scores = jnp.einsum('qhd,khd->hqk', query_rows, key_rows) / math.sqrt(HD)
        allowed = (query_docs[:, None] == doc_ids[None, :]) & ((positions[None, :] <= query_pos[:, None]) | (blocks[None, :] == query_blocks[:, None]) & query_image[:, None])
        scores = jnp.where(allowed[None], scores, masked_score)
        row_max = lax.optimization_barrier(jnp.max(scores, axis=2, keepdims=True))
        expo = jnp.where(allowed[None], jnp.exp(scores - row_max), 0.0)
        totals = lax.optimization_barrier(jnp.sum(expo, axis=2))
        weights = expo.astype(jnp.bfloat16).astype(jnp.float32)
        summed = jnp.einsum('hqk,khd->qhd', weights, value_rows)
        attended_block = summed / jnp.transpose(totals)[:, :, None]
        return attended_block.astype(jnp.bfloat16).reshape(block_len, HEADS * HD)
    starts = jnp.arange(S // block_len, dtype=jnp.int32) * block_len
    attended = lax.map(query_block, starts).reshape(S, HEADS * HD)
    group_width = HEADS * HD // N_TP
    added = residual.astype(jnp.float32)
    for group in range(N_TP):
        term = jnp.dot(attended[:, group * group_width:(group + 1) * group_width], w_out[group * group_width:(group + 1) * group_width], preferred_element_type=jnp.float32).astype(jnp.bfloat16)
        term = lax.optimization_barrier(term)
        added = added + term.astype(jnp.float32)
    hidden_out = added.astype(jnp.bfloat16)
    predicted = jnp.dot(hidden_out, w_dec, preferred_element_type=jnp.float32)
    noise_rows = jnp.zeros((n_blocks, PATCHES, PV), jnp.float32).at[image_block].set(noise.astype(jnp.float32)).reshape(S, PV)
    image_rows = image_flags[blocks] == 1
    diff = predicted - noise_rows
    patch_error = jnp.where(image_rows, lax.optimization_barrier(jnp.mean(diff * diff, axis=1)), 0.0)
    return (hidden_out, predicted, patch_error)
```

```python
import functools
import math

import jax
import jax.numpy as jnp
from jax import lax
from jax.experimental import pallas as pl
from jax.experimental.pallas import tpu as pltpu
from jax.sharding import Mesh, PartitionSpec as P

HD = 128
TSTEPS = 1000
EPS = 1e-05
PATCH_ROWS = 256
BLOCKS = 64
IMAGES = 32
TEXTS = BLOCKS - IMAGES
STRIPES = 32
SROWS = 8
NZ = 8
WIDTH = 4096
LOCAL = WIDTH // NZ
S = BLOCKS * PATCH_ROWS
DOCS = 4
SEQ_AXES = ("x", "y", "c")
MASKED = -1e30
FLOOR = -1e29
SCALE2 = math.log2(math.e) / math.sqrt(HD)
QB = 4
KB = 8
VMEM = pl.BlockSpec(memory_space=pltpu.VMEM)
SMEM = pl.BlockSpec(memory_space=pltpu.SMEM)


def shifted(a, axis, shift):
    count = lax.axis_size(axis)
    return lax.ppermute(a, axis, [(i, (i + shift) % count) for i in range(count)])


def ring_eight(a):
    up = [a]
    down = [a]
    for _ in range(3):
        up.append(shifted(up[-1], "z", 1))
        down.append(shifted(down[-1], "z", -1))
    half = a.shape[0] // 2
    far_top = shifted(up[-1][:half], "z", 1)
    far_low = shifted(down[-1][half:], "z", -1)
    return up, down[1:], (far_top, far_low)


def nt_dot(a, b):
    return lax.dot_general(a, b, (((1,), (1,)), ((), ())), preferred_element_type=jnp.float32)


def qkv_kernel(
    sc_ref, slot_ref, u0, u1, u2, u3, d1, d2, d3, f0, f1, w_ref, gain_ref, wg_ref, noised_ref,
    mine_ref, other_ref, dec_ref, res_ref, acc_ref, dec_acc,
):
    z = sc_ref[3]
    c = sc_ref[2]
    rows_t = TEXTS * SROWS
    rows = BLOCKS * SROWS
    squares = jnp.zeros((rows, 1), jnp.float32)
    decoded = jnp.zeros((rows, 64), jnp.float32)
    shifts = (0, 1, 2, 3, -1, -2, -3, 4)
    refs = (u0, u1, u2, u3, d1, d2, d3, None)
    for k, (shift, ref) in enumerate(zip(shifts, refs)):
        src = lax.rem(z - shift + NZ, NZ)
        if ref is None:
            block = jnp.concatenate([f0[...], f1[...]], axis=0)
        else:
            block = ref[...]
        text = block[:rows_t]
        times = block[rows_t:].astype(jnp.float32)
        wp = wg_ref[src, 0:64, :]
        wd = wg_ref[src, 64:128, :]
        patch = jnp.dot(noised_ref[...], wp, preferred_element_type=jnp.float32)
        timed = jnp.broadcast_to(times[:, None, :], (IMAGES, SROWS, LOCAL)).reshape(
            IMAGES * SROWS, LOCAL
        )
        image = (patch + timed).astype(jnp.bfloat16)
        both = jnp.concatenate([text, image], axis=0)
        res_ref[k] = both
        wide = both.astype(jnp.float32)
        squares = squares + jnp.sum(wide * wide, axis=1, keepdims=True)
        decoded = decoded + nt_dot(both, wd)
    dec_acc[...] = decoded
    inverse = lax.rsqrt(squares * (1.0 / WIDTH) + EPS)
    total = None
    for k, shift in enumerate(shifts):
        src = lax.rem(z - shift + NZ, NZ)
        normed = (res_ref[k].astype(jnp.float32) * inverse * gain_ref[src]).astype(jnp.bfloat16)
        part = jnp.dot(normed, w_ref[src], preferred_element_type=jnp.float32)
        total = part if total is None else total + part
    for j in range(6):
        acc_ref[j] = total[:, j * HD : (j + 1) * HD]

    def arrange(pair, carry):
        first = pl.multiple_of(slot_ref[2 * pair] * SROWS, SROWS)
        second = pl.multiple_of(slot_ref[2 * pair + 1] * SROWS, SROWS)
        at = pl.ds(pl.multiple_of(pair * 2 * SROWS, 2 * SROWS), 2 * SROWS)
        for j in range(3):
            for ref, head in ((mine_ref, c), (other_ref, 1 - c)):
                index = 2 * j + head
                ref[j, at, :] = jnp.concatenate(
                    [acc_ref[index, pl.ds(first, SROWS), :], acc_ref[index, pl.ds(second, SROWS), :]],
                    axis=0,
                ).astype(jnp.bfloat16)
        dec_ref[pair] = jnp.concatenate(
            [dec_acc[pl.ds(first, SROWS), :], dec_acc[pl.ds(second, SROWS), :]], axis=1
        )
        return carry

    lax.fori_loop(0, BLOCKS // 2, arrange, 0)


def attend_kernel(
    sc_ref, start_ref, flag_ref, q0, q1, q2, q3, kv0, kv1, kv3, k2, v2, dec_ref, img_ref,
    out_ref, qs, ks, vs, m_ref, acc_ref,
):
    x, y, c = sc_ref[0], sc_ref[1], sc_ref[2]
    ones = jnp.ones((8, 512, HD), jnp.bfloat16)
    vs[:, :, HD:] = ones
    for i in range(2):
        cc = c if i == 0 else 1 - c
        for ref, shift in ((q0, 0), (q1, 1), (q2, 2), (q3, 3)):
            qs[lax.rem(y - shift + 4, 4) * 2 + cc] = ref[i]
        for ref, shift in ((kv0, 0), (kv1, 1), (kv3, 3)):
            at = lax.rem(x - shift + 4, 4) * 2 + cc
            ks[at] = ref[i, 0]
            vs[at, :, :HD] = ref[i, 1]
        at = lax.rem(x + 2, 4) * 2 + cc
        ks[at] = k2[i]
        vs[at, :, :HD] = v2[i]

    rows = QB * 64
    cols = KB * 64
    starts = [start_ref[d] for d in range(DOCS)]

    def doc_low(position):
        low = 0
        for start in starts:
            low = jnp.where(start <= position, jnp.maximum(start, low), low)
        return low

    def q_tile(i, carry):
        rho = lax.broadcasted_iota(jnp.int32, (rows, HD), 0)
        piece, blk, row = rho >> 5, (rho >> 3) & 3, rho & 7
        first = (QB * i + blk) * PATCH_ROWS
        q_pos = first + 64 * x + 8 * piece + row
        low = jnp.zeros((rows, HD), jnp.int32)
        high_doc = jnp.full((rows, HD), S - 1, jnp.int32)
        for start in starts:
            low = jnp.where(start <= q_pos, jnp.maximum(low, start), low)
            high_doc = jnp.where(start > q_pos, jnp.minimum(high_doc, start - 1), high_doc)
        flag = jnp.zeros((rows, HD), jnp.int32)
        for n in range(QB):
            flag = jnp.where(blk == n, flag_ref[QB * i + n], flag)
        high = jnp.where(flag == 1, jnp.minimum(high_doc, first + PATCH_ROWS - 1), q_pos)
        low_col, high_col = low[:, :1], high[:, :1]
        m_ref[...] = jnp.full((rows, HD), FLOOR, jnp.float32)
        acc_ref[...] = jnp.zeros((rows, 2 * HD), jnp.float32)
        q_at = pl.ds(pl.multiple_of(i * QB * SROWS, QB * SROWS), QB * SROWS)
        low_first = doc_low(i * (QB * PATCH_ROWS))
        low_last = doc_low(i * (QB * PATCH_ROWS) + QB * PATCH_ROWS - 1)
        last = (i * QB) // KB

        def k_tile(j, inner):
            k_at = pl.ds(pl.multiple_of(j * KB * SROWS, KB * SROWS), KB * SROWS)
            full = jnp.logical_and(j < last, low_last <= j * (KB * PATCH_ROWS))

            def fold(masked):
                q = qs[:, q_at, :].reshape(rows, HD)
                k = ks[:, k_at, :].reshape(cols, HD)
                s = nt_dot(q, k)
                if masked:
                    kappa = lax.broadcasted_iota(jnp.int32, (1, cols), 1)
                    k_pos = (
                        (KB * j + ((kappa >> 3) & 7)) * PATCH_ROWS
                        + 64 * (kappa >> 7) + 16 * y + 8 * ((kappa >> 6) & 1) + (kappa & 7)
                    )
                    seen = jnp.logical_and(k_pos >= low_col, k_pos <= high_col)
                    s = jnp.where(seen, s, MASKED)
                m_old = m_ref[...]
                m_new = jnp.maximum(m_old, jnp.max(s, axis=1, keepdims=True))
                m_ref[...] = m_new
                p = jnp.exp2((s - m_new[:, :1]) * SCALE2).astype(jnp.bfloat16)
                alpha = jnp.exp2((m_old - m_new) * SCALE2)
                pv = jnp.dot(
                    p, vs[:, k_at, :].reshape(cols, 2 * HD), preferred_element_type=jnp.float32
                )
                acc_ref[...] = acc_ref[...] * jnp.concatenate([alpha, alpha], axis=1) + pv

            @pl.when(full)
            def _():
                fold(False)

            @pl.when(jnp.logical_not(full))
            def _():
                fold(True)

            return inner

        lax.fori_loop(low_first // (KB * PATCH_ROWS), last + 1, k_tile, 0)
        total = acc_ref[:, HD:]
        some = total > 0.0
        safe = jnp.where(some, total, 1.0)
        o = (acc_ref[:, :HD] / safe).astype(jnp.bfloat16).reshape(8, QB * SROWS, HD)
        level = jnp.where(some, m_ref[...] * SCALE2 + jnp.log2(safe), MASKED)
        level = level.reshape(8, QB * SROWS, HD)
        which = lax.broadcasted_iota(jnp.int32, (8, HD), 0)
        for d in range(QB // 2):
            dest = (QB // 2) * i + d
            out_ref[dest, 0:8] = o[:, 16 * d : 16 * d + 16, :]
            line = jnp.transpose(level[:, 16 * d : 16 * d + 16, :].reshape(HD, HD))[:8]
            high_part = line.astype(jnp.bfloat16).astype(jnp.float32)
            rest = line - high_part
            mid_part = rest.astype(jnp.bfloat16).astype(jnp.float32)
            low_part = rest - mid_part
            head = jnp.where(which == 0, high_part, jnp.where(which == 1, mid_part, low_part))
            out_ref[dest, 8] = jnp.concatenate([head, dec_ref[dest]], axis=0).astype(jnp.bfloat16)
            out_ref[dest, 9] = img_ref[dest]
        return carry

    lax.fori_loop(0, BLOCKS // QB, q_tile, 0)


def combine_kernel(in_ref, w2_ref, att_ref, dec_ref, full_ref):
    for x in range(4):
        for c in range(2):
            heads = [in_ref[x * 8 + y * 2 + c, 8].astype(jnp.float32) for y in range(4)]
            levels = [h[0:1] + h[1:2] + h[2:3] for h in heads]
            top = functools.reduce(jnp.maximum, levels)
            weights = [jnp.exp2(level - top) for level in levels]
            total = functools.reduce(jnp.add, weights)
            part = None
            for y in range(4):
                share = jnp.transpose(jnp.broadcast_to(weights[y] / total, (HD, HD)))
                o = in_ref[x * 8 + y * 2 + c, 0:8].reshape(HD, HD).astype(jnp.float32)
                part = o * share if part is None else part + o * share
            for p in range(8):
                for b in range(2):
                    full_ref[
                        b * PATCH_ROWS + 64 * x + 8 * p : b * PATCH_ROWS + 64 * x + 8 * p + 8,
                        c * HD : (c + 1) * HD,
                    ] = part[(2 * p + b) * 8 : (2 * p + b) * 8 + 8]
            for y in range(4):
                stripe = x * 8 + y * 2 + c
                for b in range(2):
                    at = b * PATCH_ROWS + stripe * SROWS
                    dec_ref[at : at + SROWS, :] = heads[y][8:16, b * 64 : (b + 1) * 64]
    att_ref[0:512, :] = full_ref[...].astype(jnp.bfloat16)
    att_ref[512:576, :] = w2_ref[...]


def kernel_params(mib):
    return pltpu.CompilerParams(vmem_limit_bytes=mib * 1024 * 1024)


def per_device(
    text_embed, latents, noise, timesteps, image_block, doc_ids, norm_gain,
    w_patch, w_time, w_qkv, w_out, w_dec,
):
    ix, iy, ic, iz = (lax.axis_index(a) for a in ("x", "y", "c", "z"))
    seq = ix * 8 + iy * 2 + ic
    f32, bf16 = jnp.float32, jnp.bfloat16
    scalars = jnp.stack([ix, iy, ic, iz]).astype(jnp.int32)

    out_slice = lax.dynamic_slice_in_dim(w_out, seq * 8, 8, 0).reshape(64, LOCAL)
    packed = jnp.concatenate([w_patch, w_dec.T, out_slice], axis=0)
    wg = lax.all_gather(packed, "z", axis=0, tiled=False)

    step = timesteps.astype(f32)
    signal = jnp.cos((step / TSTEPS + 0.008) / 1.008 * (math.pi / 2)) ** 2
    noised = (
        jnp.sqrt(signal)[:, None, None] * latents.astype(f32)
        + jnp.sqrt(1.0 - signal)[:, None, None] * noise.astype(f32)
    ).astype(bf16)
    freq_count = w_time.shape[0] // 2
    freqs = jnp.exp(-math.log(10000.0) * jnp.arange(freq_count, dtype=f32) / freq_count)
    angles = step[:, None] * freqs[None, :]
    feats = jnp.concatenate([jnp.cos(angles), jnp.sin(angles)], axis=1).astype(bf16)

    text_part = (
        text_embed.reshape(2, STRIPES, SROWS, LOCAL)
        .transpose(1, 0, 2, 3)
        .reshape(STRIPES, 2 * SROWS, LOCAL)
    )
    feat_row = jnp.pad(feats, ((0, 0), (0, 256)))
    image_part = jnp.stack(
        [
            noised.reshape(STRIPES, 512),
            noise.reshape(STRIPES, 512),
            jnp.broadcast_to(feat_row, (STRIPES, 512)),
            jnp.zeros((STRIPES, 512), bf16),
        ],
        axis=1,
    )
    sent = jnp.concatenate([text_part, image_part], axis=1)
    got = lax.all_to_all(sent, SEQ_AXES, 0, 0, tiled=False)

    block_ids = jnp.arange(BLOCKS, dtype=jnp.int32)
    matches = image_block[None, :] == block_ids[:, None]
    flags = jnp.any(matches, axis=1)
    image_of = jnp.sum(jnp.where(matches, jnp.arange(IMAGES, dtype=jnp.int32)[None, :], 0), axis=1)
    rank = jnp.sum(
        jnp.where((block_ids[None, :] < block_ids[:, None]) & ~flags[None, :], 1, 0), axis=1
    )
    slots = jnp.where(flags, TEXTS + image_of, rank).astype(jnp.int32)
    text_ids = jnp.arange(TEXTS, dtype=jnp.int32)
    text_block = jnp.sum(
        jnp.where((rank[None, :] == text_ids[:, None]) & ~flags[None, :], block_ids[None, :], 0),
        axis=1,
    )
    doc_start = jnp.sum(
        (doc_ids[None, :] < jnp.arange(DOCS, dtype=jnp.int32)[:, None]).astype(jnp.int32), axis=1
    )
    flag_ints = flags.astype(jnp.int32)

    text_rows = got[:, :16].reshape(BLOCKS, SROWS, LOCAL)[text_block].reshape(-1, LOCAL)
    every_feats = got[:, 18, :256]
    time_part = jnp.dot(every_feats, w_time, preferred_element_type=f32)
    payload = jnp.concatenate([text_rows, time_part.astype(bf16)], axis=0)
    up, down, far = ring_eight(payload)

    noised_rows = got[:, 16].reshape(IMAGES * SROWS, 64)
    noise_rows = got[:, 17].reshape(IMAGES * SROWS, 64)
    pair_rows = jnp.concatenate([noised_rows, noise_rows], axis=1).reshape(IMAGES, SROWS, 128)
    image_back = pair_rows[image_of].reshape(STRIPES, 2 * SROWS, 128)

    w_cols, _ = lax.optimization_barrier((w_qkv, got))
    w_cols = w_cols.reshape(NZ, LOCAL, 6 * HD)
    gains = norm_gain.reshape(NZ, 1, LOCAL)

    mine, other, dec_rows = pl.pallas_call(
        qkv_kernel,
        out_shape=(
            jax.ShapeDtypeStruct((3, BLOCKS * SROWS, HD), bf16),
            jax.ShapeDtypeStruct((3, BLOCKS * SROWS, HD), bf16),
            jax.ShapeDtypeStruct((STRIPES, SROWS, 128), f32),
        ),
        in_specs=[SMEM, SMEM] + [VMEM] * 13,
        out_specs=(VMEM, VMEM, VMEM),
        scratch_shapes=[
            pltpu.VMEM((NZ, BLOCKS * SROWS, LOCAL), bf16),
            pltpu.VMEM((6, BLOCKS * SROWS, HD), f32),
            pltpu.VMEM((BLOCKS * SROWS, 64), f32),
        ],
        compiler_params=kernel_params(48),
        name="qkv",
    )(scalars, slots, *up, *down, *far, w_cols, gains, wg, noised_rows)

    theirs = lax.ppermute(other, "c", [(0, 1), (1, 0)])
    pieces = jnp.stack([mine, theirs])
    q = pieces[:, 0]
    kv = pieces[:, 1:]
    k = pieces[:, 1]
    v = pieces[:, 2]
    q1, q3 = shifted(q, "y", 1), shifted(q, "y", -1)
    kv1, kv3 = shifted(kv, "x", 1), shifted(kv, "x", -1)
    q2 = shifted(q, "y", 2)
    k2, v2 = shifted(k, "x", 2), shifted(v, "x", 2)

    partial = pl.pallas_call(
        attend_kernel,
        out_shape=jax.ShapeDtypeStruct((STRIPES, 10, 16, HD), bf16),
        in_specs=[SMEM, SMEM, SMEM] + [VMEM] * 11,
        out_specs=VMEM,
        scratch_shapes=[
            pltpu.VMEM((8, 512, HD), bf16),
            pltpu.VMEM((8, 512, HD), bf16),
            pltpu.VMEM((8, 512, 2 * HD), bf16),
            pltpu.VMEM((QB * 64, HD), f32),
            pltpu.VMEM((QB * 64, 2 * HD), f32),
        ],
        compiler_params=kernel_params(48),
        name="attend",
    )(scalars, doc_start, flag_ints, q, q1, q2, q3, kv, kv1, kv3, k2, v2, dec_rows, image_back)
    parts = lax.all_to_all(partial, SEQ_AXES, 0, 0, tiled=False)

    own = lax.dynamic_index_in_dim(wg[:, 128:].reshape(NZ, 8, NZ, LOCAL), iz, 2, keepdims=False)
    out_cols = lax.all_gather(own, SEQ_AXES, axis=0, tiled=False)
    out_cols = out_cols.transpose(1, 0, 2, 3).reshape(NZ, 2 * HD, LOCAL)
    w_dec_t = wg[:, 64:128].transpose(1, 0, 2).reshape(64, WIDTH)
    w2_t = nt_dot(w_dec_t, w_out).astype(bf16)

    att, dec_own = pl.pallas_call(
        combine_kernel,
        out_shape=(
            jax.ShapeDtypeStruct((576, 2 * HD), bf16),
            jax.ShapeDtypeStruct((512, 64), f32),
        ),
        in_specs=[VMEM, VMEM],
        out_specs=(VMEM, VMEM),
        scratch_shapes=[pltpu.VMEM((512, 2 * HD), f32)],
        compiler_params=kernel_params(32),
        name="combine",
    )(parts, w2_t)

    up, down, far = ring_eight(att)
    own_images = (
        parts[:, 9].reshape(STRIPES, 2, SROWS, 128).transpose(1, 0, 2, 3).reshape(512, 128)
    )
    own_noised, own_noise = own_images[:, :64], own_images[:, 64:].astype(f32)
    own_blocks = 2 * seq + jnp.arange(2, dtype=jnp.int32)
    own_times = time_part[image_of[own_blocks]]
    own_flags = flags[own_blocks]
    embedded = (
        jnp.dot(own_noised, w_patch, preferred_element_type=f32).reshape(2, PATCH_ROWS, LOCAL)
        + own_times[:, None, :]
    ).astype(bf16)
    residual = jnp.where(
        own_flags[:, None, None], embedded, text_embed.reshape(2, PATCH_ROWS, LOCAL)
    ).reshape(512, LOCAL)

    blocks = list(zip(up, (0, 1, 2, 3))) + list(zip(down, (-1, -2, -3)))
    blocks.append((jnp.concatenate(far, axis=0), 4))
    hidden = residual.astype(f32)
    predicted = dec_own
    for block, shift in blocks:
        src = lax.rem(iz - shift + NZ, NZ)
        w_part = lax.dynamic_index_in_dim(out_cols, src, 0, keepdims=False)
        hidden = hidden + jnp.dot(block[:512], w_part, preferred_element_type=f32)
        predicted = predicted + nt_dot(block[:512], block[512:])
    hidden_out = hidden.astype(bf16)
    difference = predicted - own_noise
    error = jnp.mean(difference * difference, axis=1).reshape(2, PATCH_ROWS)
    patch_error = jnp.where(own_flags[:, None], error, 0.0).reshape(512)
    return hidden_out, predicted, patch_error


def solution(mesh):
    fine = Mesh(mesh.devices.reshape(4, 4, 2, NZ), ("x", "y", "c", "z"))
    seq, tp = SEQ_AXES, "z"
    in_specs = (
        P(seq, tp),
        P(seq, None, None),
        P(seq, None, None),
        P(seq),
        P(),
        P(),
        P(),
        P(None, tp),
        P(None, tp),
        P(None, None, tp),
        P(tp, None),
        P(tp, None),
    )
    out_specs = (P(seq, tp), P(seq, None), P(seq))
    return jax.shard_map(
        per_device, mesh=fine, in_specs=in_specs, out_specs=out_specs, check_vma=False
    )
```

```python
import functools
import math

import jax
import jax.numpy as jnp
from jax import lax
from jax.experimental import pallas as pl
from jax.experimental.pallas import tpu as pltpu
from jax.sharding import Mesh, PartitionSpec as P

HD = 128
TSTEPS = 1000
EPS = 1e-05
PATCH_ROWS = 256
BLOCKS = 64
IMAGES = 32
TEXTS = BLOCKS - IMAGES
STRIPES = 32
SROWS = 8
NZ = 8
WIDTH = 4096
LOCAL = WIDTH // NZ
S = BLOCKS * PATCH_ROWS
DOCS = 4
SEQ_AXES = ("x", "y", "c")
MASKED = -1e30
FLOOR = -1e29
SCALE2 = math.log2(math.e) / math.sqrt(HD)
QB = 16
KB = 16
TEXT_ROWS = TEXTS * SROWS
ROWS = BLOCKS * SROWS
VMEM = pl.BlockSpec(memory_space=pltpu.VMEM)
SMEM = pl.BlockSpec(memory_space=pltpu.SMEM)
ANY = pl.BlockSpec(memory_space=pl.ANY)


def shifted(a, axis, shift):
    count = lax.axis_size(axis)
    return lax.ppermute(a, axis, [(i, (i + shift) % count) for i in range(count)])


def ring_step(up, down):
    return shifted(up, "z", 1), shifted(down, "z", -1)


def ring_end(up, down):
    half = up.shape[0] // 2
    return shifted(up[:half], "z", 1), shifted(down[half:], "z", -1)


def nt_dot(a, b):
    return lax.dot_general(a, b, (((1,), (1,)), ((), ())), preferred_element_type=jnp.float32)


def pack_kernel(coef_ref, text_ref, clean_ref, noise_ref, feat_ref, out_ref):
    noise = noise_ref[...].astype(jnp.float32)
    noised = coef_ref[0] * clean_ref[...].astype(jnp.float32) + coef_ref[1] * noise
    pairs = jnp.transpose(jnp.concatenate([noised, noise], axis=0))
    feats = jnp.concatenate(
        [feat_ref[0:1, :HD], feat_ref[0:1, HD:], jnp.zeros((6, HD), jnp.float32)], axis=0
    )
    for s in range(0, STRIPES, 2):
        rows = [
            text_ref[b * PATCH_ROWS + s * SROWS : b * PATCH_ROWS + (s + 2) * SROWS, :].astype(
                jnp.float32
            )
            for b in range(2)
        ]
        for n in range(2):
            at = n * SROWS
            out_ref[s + n, :, :LOCAL] = jnp.concatenate(
                [rows[0][at : at + SROWS], rows[1][at : at + SROWS]], axis=0
            ).astype(jnp.bfloat16)
            patch = pairs[(s + n) * SROWS : (s + n + 1) * SROWS]
            out_ref[s + n, :, LOCAL:] = jnp.concatenate([patch, feats], axis=0).astype(jnp.bfloat16)


def sort_kernel(
    sc_ref, image_ref, doc_ref, got_ref, wt_ref,
    pay_ref, noised_ref, back_ref, times_ref, slot_ref, flag_ref, start_ref, text_ref, both_ref,
):
    seq = sc_ref[4]

    def clear(b, carry):
        flag_ref[b] = 0
        slot_ref[b] = 0
        return carry

    lax.fori_loop(0, BLOCKS, clear, 0)

    def mark(i, carry):
        block = image_ref[i]
        flag_ref[block] = 1
        slot_ref[block] = TEXTS + i
        return carry

    lax.fori_loop(0, IMAGES, mark, 0)
    docs = doc_ref[...]
    for d in range(DOCS):
        start_ref[d] = jnp.sum((docs < d).astype(jnp.int32))

    feats = jnp.concatenate(
        [got_ref[i, :, LOCAL:].astype(jnp.float32)[8:10].reshape(1, 2, HD) for i in range(IMAGES)],
        axis=0,
    )
    first, second = feats[:, 0, :].astype(jnp.bfloat16), feats[:, 1, :].astype(jnp.bfloat16)
    times = jnp.dot(first, wt_ref[:HD], preferred_element_type=jnp.float32) + jnp.dot(
        second, wt_ref[HD:], preferred_element_type=jnp.float32
    )
    both_ref[...] = times
    for n in range(2):
        image = jnp.maximum(slot_ref[2 * seq + n] - TEXTS, 0)
        times_ref[n : n + 1, :] = both_ref[pl.ds(image, 1), :]
    pay_ref[TEXT_ROWS:, :] = times.astype(jnp.bfloat16)

    def place(pair, rank):
        wide = got_ref[pair, :, :LOCAL].astype(jnp.float32)
        for n in range(2):
            b = 2 * pair + n
            is_text = flag_ref[b] == 0

            @pl.when(is_text)
            def _(b=b, n=n, rank=rank):
                slot_ref[b] = rank
                text_ref[pl.ds(pl.multiple_of(rank * SROWS, SROWS), SROWS), :] = wide[
                    n * SROWS : (n + 1) * SROWS
                ]

            rank = rank + jnp.where(is_text, 1, 0)
        return rank

    lax.fori_loop(0, BLOCKS // 2, place, 0)
    pay_ref[:TEXT_ROWS, :] = text_ref[...].astype(jnp.bfloat16)

    for i in range(0, IMAGES, 2):
        pair = jnp.concatenate(
            [got_ref[i + n, :, LOCAL:].astype(jnp.float32)[:SROWS] for n in range(2)], axis=0
        )
        noised_ref[i * SROWS : (i + 2) * SROWS, :] = pair[:, :64].astype(jnp.bfloat16)

    def back(pair, carry):
        parts = [
            got_ref[jnp.maximum(slot_ref[2 * pair + n] - TEXTS, 0), :, LOCAL:].astype(jnp.float32)[
                :SROWS
            ]
            for n in range(2)
        ]
        back_ref[pair] = jnp.concatenate(parts, axis=0).astype(jnp.bfloat16)
        return carry

    lax.fori_loop(0, BLOCKS // 2, back, 0)


def fold_chunks(
    z, shifts, chunks, w_hbm, wg_hbm, gain_ref, noised_ref, w_ref, wg_ref, sems,
    acc_ref, sq_ref, dec_ref,
):
    sources = [lax.rem(z - shift + NZ, NZ) for shift in shifts]
    copies = [
        (
            pltpu.make_async_copy(wg_hbm.at[src, 0:128], wg_ref.at[n], sems.at[0, n]),
            pltpu.make_async_copy(w_hbm.at[:, src], w_ref.at[n], sems.at[1, n]),
        )
        for n, src in enumerate(sources)
    ]
    for pair in copies:
        pair[0].start()
        pair[1].start()
    for n, (src, block) in enumerate(zip(sources, chunks)):
        times = block[TEXT_ROWS:].astype(jnp.float32)
        copies[n][0].wait()
        patch = jnp.dot(noised_ref[...], wg_ref[n, 0:64, :], preferred_element_type=jnp.float32)
        timed = jnp.broadcast_to(times[:, None, :], (IMAGES, SROWS, LOCAL))
        image = (patch + timed.reshape(IMAGES * SROWS, LOCAL)).astype(jnp.bfloat16)
        both = jnp.concatenate([block[:TEXT_ROWS], image], axis=0)
        wide = both.astype(jnp.float32)
        square = wide * wide
        sq_ref[...] += sum(square[:, g * HD : (g + 1) * HD] for g in range(LOCAL // HD))
        dec_ref[...] += nt_dot(both, wg_ref[n, 64:128, :])
        left = (wide * gain_ref[src]).astype(jnp.bfloat16)
        copies[n][1].wait()
        for j in range(3):
            acc_ref[j] += jnp.dot(left, w_ref[n, j], preferred_element_type=jnp.float32)


def part_kernel(shifts, first, sc_ref, *refs):
    n = len(shifts)
    chunks, refs = refs[:n], refs[n:]
    w_hbm, wg_hbm, gain_ref, noised_ref = refs[:4]
    refs = refs[4:]
    if not first:
        acc_in, sq_in, dec_in = refs[:3]
        refs = refs[3:]
    acc_ref, sq_ref, dec_ref, w_ref, wg_ref, sems = refs
    if first:
        acc_ref[...] = jnp.zeros(acc_ref.shape, jnp.float32)
        sq_ref[...] = jnp.zeros(sq_ref.shape, jnp.float32)
        dec_ref[...] = jnp.zeros(dec_ref.shape, jnp.float32)
    else:
        acc_ref[...] = acc_in[...]
        sq_ref[...] = sq_in[...]
        dec_ref[...] = dec_in[...]
    fold_chunks(
        sc_ref[3], shifts, [c[...] for c in chunks], w_hbm, wg_hbm, gain_ref, noised_ref,
        w_ref, wg_ref, sems, acc_ref, sq_ref, dec_ref,
    )


def finish_kernel(
    sc_ref, slot_ref, f0, f1, w_hbm, wg_hbm, gain_ref, noised_ref, acc_in, sq_in, dec_in,
    my_q, my_kv, their_q, their_kv, dec_out,
    acc_ref, sq_ref, dec_ref, w_ref, wg_ref, sems, six_ref,
):
    c = sc_ref[2]
    acc_ref[...] = acc_in[...]
    sq_ref[...] = sq_in[...]
    dec_ref[...] = dec_in[...]
    far = jnp.concatenate([f0[...], f1[...]], axis=0)
    fold_chunks(
        sc_ref[3], (4,), [far], w_hbm, wg_hbm, gain_ref, noised_ref,
        w_ref, wg_ref, sems, acc_ref, sq_ref, dec_ref,
    )
    squares = jnp.sum(sq_ref[...], axis=1, keepdims=True)
    inverse = lax.rsqrt(squares * (1.0 / WIDTH) + EPS)
    for j in range(3):
        scale = inverse * SCALE2 if j == 0 else inverse
        for h in range(2):
            six_ref[2 * j + h] = acc_ref[j, :, h * HD : (h + 1) * HD] * scale

    def arrange(pair, carry):
        first = pl.multiple_of(slot_ref[2 * pair] * SROWS, SROWS)
        second = pl.multiple_of(slot_ref[2 * pair + 1] * SROWS, SROWS)
        at = pl.ds(pl.multiple_of(pair * 2 * SROWS, 2 * SROWS), 2 * SROWS)

        def rows_of(index):
            return jnp.concatenate(
                [six_ref[index, pl.ds(first, SROWS), :], six_ref[index, pl.ds(second, SROWS), :]],
                axis=0,
            ).astype(jnp.bfloat16)

        for q_ref, kv_ref, head in ((my_q, my_kv, c), (their_q, their_kv, 1 - c)):
            q_ref[at, :] = rows_of(head)
            kv_ref[0, at, :] = rows_of(2 + head)
            kv_ref[1, at, :] = rows_of(4 + head)
        dec_out[pair] = jnp.concatenate(
            [dec_ref[pl.ds(first, SROWS), :], dec_ref[pl.ds(second, SROWS), :]], axis=1
        )
        return carry

    lax.fori_loop(0, BLOCKS // 2, arrange, 0)


def attend_kernel(
    sc_ref, start_ref, flag_ref, q0, q1, q2, q3, kv0, kv1, kv3, k2, v2, dec_ref, img_ref,
    out_ref, qs, ks, vs, vx, m_ref, acc_ref, sems,
):
    x, y, c = sc_ref[0], sc_ref[1], sc_ref[2]
    copies = []

    def bring(source, target):
        copy = pltpu.make_async_copy(source, target, sems.at[len(copies)])
        copy.start()
        copies.append(copy)

    for i in range(2):
        cc = c if i == 0 else 1 - c
        for ref, shift in ((kv0, 0), (kv1, 1), (kv3, 3)):
            at = lax.rem(x - shift + 4, 4) * 2 + cc
            bring(ref.at[i, 1], vs.at[at])
            bring(ref.at[i, 0], ks.at[at])
        at = lax.rem(x + 2, 4) * 2 + cc
        bring(v2.at[i], vs.at[at])
        bring(k2.at[i], ks.at[at])
        for ref, shift in ((q0, 0), (q1, 1), (q2, 2), (q3, 3)):
            bring(ref.at[i], qs.at[:, lax.rem(y - shift + 4, 4) * 2 + cc])
    for copy in copies:
        copy.wait()
    for p in range(8):
        vx[p, :HD, :] = jnp.transpose(vs[p].astype(jnp.float32)).astype(jnp.bfloat16)
        vx[p, HD:, :] = jnp.ones((16, ROWS), jnp.bfloat16)

    rows = QB * 64
    cols = KB * 64
    tile = KB * PATCH_ROWS
    starts = [start_ref[d] for d in range(DOCS)]

    def doc_low(position):
        low = 0
        for start in starts:
            low = jnp.where(start <= position, jnp.maximum(start, low), low)
        return low

    def q_tile(i, carry):
        rho = lax.broadcasted_iota(jnp.int32, (8, rows), 1)
        blk = 2 * (rho >> 7) + ((rho >> 3) & 1)
        first = (QB * i + blk) * PATCH_ROWS
        q_pos = first + 64 * x + 8 * ((rho >> 4) & 7) + (rho & 7)
        low = jnp.zeros((8, rows), jnp.int32)
        high_doc = jnp.full((8, rows), S - 1, jnp.int32)
        for start in starts:
            low = jnp.where(start <= q_pos, jnp.maximum(low, start), low)
            high_doc = jnp.where(start > q_pos, jnp.minimum(high_doc, start - 1), high_doc)
        flag = jnp.zeros((8, rows), jnp.int32)
        for n in range(QB):
            flag = jnp.where(blk == n, flag_ref[QB * i + n], flag)
        high = jnp.where(flag == 1, jnp.minimum(high_doc, first + PATCH_ROWS - 1), q_pos)
        low_line, high_line = low[:1], high[:1]
        m_ref[...] = jnp.full((8, rows), FLOOR, jnp.float32)
        acc_ref[...] = jnp.zeros((HD + 16, rows), jnp.float32)
        dests = QB // 2
        q_at = pl.ds(i * dests, dests)
        low_first = doc_low(i * (QB * PATCH_ROWS))
        low_last = doc_low(i * (QB * PATCH_ROWS) + QB * PATCH_ROWS - 1)
        begin = low_first // tile
        clear = jnp.minimum((low_last + tile - 1) // tile, i)

        def fold(j, masked):
            k_at = pl.ds(pl.multiple_of(j * KB * SROWS, KB * SROWS), KB * SROWS)
            k = ks[:, k_at, :].reshape(cols, HD)
            v = jnp.concatenate([vx[p, :, k_at] for p in range(8)], axis=1)
            q = qs[q_at].reshape(rows, HD)
            s = nt_dot(k, q)
            if masked:
                kappa = lax.broadcasted_iota(jnp.int32, (cols, 1), 0)
                k_pos = (
                    (KB * j + ((kappa >> 3) & 15)) * PATCH_ROWS
                    + 64 * (kappa >> 8) + 16 * y + 8 * ((kappa >> 7) & 1) + (kappa & 7)
                )
                seen = jnp.logical_and(k_pos >= low_line, k_pos <= high_line)
                s = jnp.where(seen, s, MASKED)
            m_old = m_ref[0:1]
            m_new = jnp.maximum(m_old, jnp.max(s, axis=0, keepdims=True))
            m_ref[0:1] = m_new
            p = jnp.exp2(s - m_new).astype(jnp.bfloat16)
            alpha = jnp.exp2(m_old - m_new)
            acc_ref[...] = acc_ref[...] * alpha + jnp.dot(v, p, preferred_element_type=jnp.float32)
            return 0

        lax.fori_loop(begin, clear, lambda j, _: fold(j, True), 0)
        lax.fori_loop(clear, i, lambda j, _: fold(j, False), 0)
        fold(i, True)

        total = acc_ref[HD : HD + 1]
        some = total > 0.0
        safe = jnp.where(some, total, 1.0)
        o = jnp.transpose(acc_ref[:HD] / safe).astype(jnp.bfloat16)
        level = jnp.where(some, m_ref[0:1] + jnp.log2(safe), MASKED)
        high_part = level.astype(jnp.bfloat16).astype(jnp.float32)
        rest = level - high_part
        mid_part = rest.astype(jnp.bfloat16).astype(jnp.float32)
        low_part = rest - mid_part
        head = jnp.concatenate(
            [high_part, mid_part, low_part, jnp.zeros((5, rows), jnp.float32)], axis=0
        )
        for d in range(dests):
            dest = dests * i + d
            out_ref[dest, 0:8] = o[HD * d : HD * (d + 1)].reshape(8, 16, HD)
            out_ref[dest, 8] = jnp.concatenate(
                [head[:, HD * d : HD * (d + 1)], dec_ref[dest]], axis=0
            ).astype(jnp.bfloat16)
            out_ref[dest, 9] = img_ref[dest]
        return carry

    lax.fori_loop(0, BLOCKS // QB, q_tile, 0)


def combine_kernel(in_ref, w2_ref, att_ref, dec_ref, full_ref):
    for x in range(4):
        for c in range(2):
            heads = [in_ref[x * 8 + y * 2 + c, 8].astype(jnp.float32) for y in range(4)]
            levels = [h[0:1] + h[1:2] + h[2:3] for h in heads]
            top = functools.reduce(jnp.maximum, levels)
            weights = [jnp.exp2(level - top) for level in levels]
            total = functools.reduce(jnp.add, weights)
            part = None
            for y in range(4):
                share = jnp.transpose(jnp.broadcast_to(weights[y] / total, (HD, HD)))
                o = in_ref[x * 8 + y * 2 + c, 0:8].reshape(HD, HD).astype(jnp.float32)
                part = o * share if part is None else part + o * share
            for p in range(8):
                for b in range(2):
                    full_ref[
                        b * PATCH_ROWS + 64 * x + 8 * p : b * PATCH_ROWS + 64 * x + 8 * p + 8,
                        c * HD : (c + 1) * HD,
                    ] = part[(2 * p + b) * 8 : (2 * p + b) * 8 + 8]
            for y in range(4):
                stripe = x * 8 + y * 2 + c
                for b in range(2):
                    at = b * PATCH_ROWS + stripe * SROWS
                    dec_ref[at : at + SROWS, :] = heads[y][8:16, b * 64 : (b + 1) * 64]
    att_ref[0:512, :] = full_ref[...].astype(jnp.bfloat16)
    att_ref[512:576, :] = w2_ref[...]


def project_chunks(z, shifts, chunks, cols_hbm, cols_ref, sems, hid_ref, pred_ref):
    copies = []
    for n, shift in enumerate(shifts):
        src = lax.rem(z - shift + NZ, NZ)
        copies.append(pltpu.make_async_copy(cols_hbm.at[src], cols_ref.at[n], sems.at[n]))
        copies[n].start()
    for n, block in enumerate(chunks):
        attended = block[:ROWS]
        pred_ref[...] += nt_dot(attended, block[ROWS:])
        copies[n].wait()
        hid_ref[...] += jnp.dot(attended, cols_ref[n], preferred_element_type=jnp.float32)


def start_kernel(
    sc_ref, flag_ref, c0, c1, c2, cols_hbm, parts_ref, text_ref, wp_ref, times_ref, dec_ref,
    hid_ref, pred_ref, noise_ref, cols_ref, sems,
):
    seq = sc_ref[4]
    for b in range(2):
        at = slice(b * PATCH_ROWS, (b + 1) * PATCH_ROWS)
        pairs = parts_ref[...].astype(jnp.float32)[:, b * SROWS : (b + 1) * SROWS].reshape(
            PATCH_ROWS, 2 * 64
        )
        noise_ref[at, :] = pairs[:, 64:]
        patch = jnp.dot(
            pairs[:, :64].astype(jnp.bfloat16), wp_ref[...], preferred_element_type=jnp.float32
        )
        image = (patch + times_ref[b : b + 1, :]).astype(jnp.bfloat16).astype(jnp.float32)
        text = text_ref[at, :].astype(jnp.float32)
        hid_ref[at, :] = jnp.where(flag_ref[2 * seq + b] == 1, image, text)
    pred_ref[...] = dec_ref[...]
    project_chunks(
        sc_ref[3], (0, 1, -1), [c0[...], c1[...], c2[...]], cols_hbm, cols_ref, sems,
        hid_ref, pred_ref,
    )


def middle_kernel(
    shifts, sc_ref, c0, c1, cols_hbm, hid_in, pred_in, hid_ref, pred_ref, cols_ref, sems
):
    hid_ref[...] = hid_in[...]
    pred_ref[...] = pred_in[...]
    project_chunks(
        sc_ref[3], shifts, [c0[...], c1[...]], cols_hbm, cols_ref, sems, hid_ref, pred_ref
    )


def close_kernel(
    sc_ref, flag_ref, f0, f1, cols_hbm, hid_in, pred_in, noise_ref,
    out_ref, pred_ref, err_ref, hid_ref, cols_ref, sems,
):
    seq = sc_ref[4]
    hid_ref[...] = hid_in[...]
    pred_ref[...] = pred_in[...]
    far = jnp.concatenate([f0[...], f1[...]], axis=0)
    project_chunks(sc_ref[3], (4,), [far], cols_hbm, cols_ref, sems, hid_ref, pred_ref)
    out_ref[...] = hid_ref[...].astype(jnp.bfloat16)
    gap = pred_ref[...] - noise_ref[...]
    square = jnp.transpose(gap * gap)
    mean = jnp.sum(square, axis=0, keepdims=True) * (1.0 / 64)
    for b in range(2):
        at = slice(b * PATCH_ROWS, (b + 1) * PATCH_ROWS)
        err_ref[0:1, at] = jnp.where(flag_ref[2 * seq + b] == 1, mean[:, at], 0.0)


def kernel_params(mib):
    return pltpu.CompilerParams(vmem_limit_bytes=mib * 1024 * 1024)


def call(kernel, name, outs, in_specs, args, scratch=(), mib=48, flops=0, nbytes=0, out_specs=None):
    return pl.pallas_call(
        kernel,
        out_shape=tuple(jax.ShapeDtypeStruct(shape, dtype) for shape, dtype in outs),
        in_specs=in_specs,
        out_specs=out_specs or tuple(VMEM for _ in outs),
        scratch_shapes=list(scratch),
        compiler_params=kernel_params(mib),
        cost_estimate=pl.CostEstimate(flops=flops, bytes_accessed=nbytes, transcendentals=0),
        name=name,
    )(*args)


def per_device(
    text_embed, latents, noise, timesteps, image_block, doc_ids, norm_gain,
    w_patch, w_time, w_qkv, w_out, w_dec,
):
    ix, iy, ic, iz = (lax.axis_index(a) for a in ("x", "y", "c", "z"))
    seq = ix * 8 + iy * 2 + ic
    f32, bf16, i32 = jnp.float32, jnp.bfloat16, jnp.int32
    scalars = jnp.stack([ix, iy, ic, iz, seq]).astype(i32)

    step = timesteps.astype(f32)
    signal = jnp.cos((step / TSTEPS + 0.008) / 1.008 * (math.pi / 2)) ** 2
    coefs = jnp.concatenate([jnp.sqrt(signal), jnp.sqrt(1.0 - signal)])
    freq_count = w_time.shape[0] // 2
    freqs = jnp.exp(-math.log(10000.0) * jnp.arange(freq_count, dtype=f32) / freq_count)
    angles = step[:, None] * freqs[None, :]
    feats = jnp.concatenate([jnp.cos(angles), jnp.sin(angles)], axis=1)
    (sent,) = call(
        pack_kernel, "pack", [((STRIPES, 2 * SROWS, LOCAL + HD), bf16)], [SMEM] + [VMEM] * 4,
        (coefs, text_embed, latents[0].T, noise[0].T, feats), mib=16,
    )
    got = lax.all_to_all(sent, SEQ_AXES, 0, 0, tiled=False)

    out_slice = lax.dynamic_slice_in_dim(w_out, seq * 8, 8, 0).reshape(64, LOCAL)
    packed = jnp.concatenate([w_patch, w_dec.T, out_slice], axis=0)
    wg = lax.all_gather(packed, "z", axis=0, tiled=False)

    payload, noised, image_back, own_times, slots, flags, starts = call(
        sort_kernel, "sort",
        [
            ((TEXT_ROWS + IMAGES, LOCAL), bf16),
            ((IMAGES * SROWS, 64), bf16),
            ((STRIPES, 2 * SROWS, HD), bf16),
            ((2, LOCAL), f32),
            ((BLOCKS,), i32),
            ((BLOCKS,), i32),
            ((DOCS,), i32),
        ],
        [SMEM, SMEM, VMEM, VMEM, VMEM],
        (scalars, image_block, doc_ids.reshape(128, 128), got, w_time),
        scratch=[pltpu.VMEM((TEXT_ROWS, LOCAL), f32), pltpu.VMEM((IMAGES, LOCAL), f32)],
        mib=16, out_specs=(VMEM,) * 4 + (SMEM,) * 3,
    )
    w_cols = w_qkv.transpose(1, 0, 2).reshape(3, NZ, LOCAL, 2 * HD)
    gains = norm_gain.reshape(NZ, 1, LOCAL)
    sums = [((3, ROWS, 2 * HD), f32), ((ROWS, HD), f32), ((ROWS, 64), f32)]

    def fold(shifts, chunks, state):
        count = len(shifts)
        return call(
            functools.partial(part_kernel, shifts, not state), "part", sums,
            [SMEM] + [VMEM] * count + [ANY] * 2 + [VMEM] * (2 + len(state)),
            (scalars, *chunks, w_cols, wg, gains, noised, *state),
            scratch=[
                pltpu.VMEM((count, 3, LOCAL, 2 * HD), bf16),
                pltpu.VMEM((count, 128, LOCAL), bf16),
                pltpu.SemaphoreType.DMA((2, count)),
            ],
            flops=count * 2 * ROWS * LOCAL * 6 * HD, nbytes=4 << 20,
        )

    up1, down1 = ring_step(payload, payload)
    up2, down2 = ring_step(up1, down1)
    up2, down2, wg = lax.optimization_barrier((up2, down2, wg))
    up3, down3 = ring_step(up2, down2)
    state = fold((0, 1, -1, 2, -2), (payload, up1, down1, up2, down2), ())
    up3, down3, *state = lax.optimization_barrier((up3, down3, *state))
    far = ring_end(up3, down3)
    state = fold((3, -3), (up3, down3), state)
    my_q, my_kv, their_q, their_kv, dec_rows = call(
        finish_kernel, "finish",
        [
            ((ROWS, HD), bf16),
            ((2, ROWS, HD), bf16),
            ((ROWS, HD), bf16),
            ((2, ROWS, HD), bf16),
            ((STRIPES, SROWS, HD), f32),
        ],
        [SMEM, SMEM, VMEM, VMEM, ANY, ANY] + [VMEM] * 5,
        (scalars, slots, *far, w_cols, wg, gains, noised, *state),
        scratch=[
            pltpu.VMEM((3, ROWS, 2 * HD), f32),
            pltpu.VMEM((ROWS, HD), f32),
            pltpu.VMEM((ROWS, 64), f32),
            pltpu.VMEM((1, 3, LOCAL, 2 * HD), bf16),
            pltpu.VMEM((1, 128, LOCAL), bf16),
            pltpu.SemaphoreType.DMA((2, 1)),
            pltpu.VMEM((6, ROWS, HD), f32),
        ],
    )

    got_q = lax.ppermute(their_q, "c", [(0, 1), (1, 0)])
    got_kv = lax.ppermute(their_kv, "c", [(0, 1), (1, 0)])
    q = jnp.stack([my_q, got_q])
    kv = jnp.stack([my_kv, got_kv])
    k, v = kv[:, 0], kv[:, 1]
    kv1, kv3 = shifted(kv, "x", 1), shifted(kv, "x", -1)
    q1, q3 = shifted(q, "y", 1), shifted(q, "y", -1)
    k2, v2 = shifted(k, "x", 2), shifted(v, "x", 2)
    q2 = shifted(q, "y", 2)
    by_dest = [a.reshape(2, STRIPES, 16, HD) for a in (q, q1, q2, q3)]

    (partial,) = call(
        attend_kernel, "attend", [((STRIPES, 10, 16, HD), bf16)],
        [SMEM] * 3 + [ANY] * 9 + [VMEM] * 2,
        (scalars, starts, flags, *by_dest, kv, kv1, kv3, k2, v2, dec_rows, image_back),
        scratch=[
            pltpu.VMEM((STRIPES, 8, 16, HD), bf16),
            pltpu.VMEM((8, ROWS, HD), bf16),
            pltpu.VMEM((8, ROWS, HD), bf16),
            pltpu.VMEM((8, HD + 16, ROWS), bf16),
            pltpu.VMEM((8, QB * 64), f32),
            pltpu.VMEM((HD + 16, QB * 64), f32),
            pltpu.SemaphoreType.DMA((24,)),
        ],
        flops=5 << 30, nbytes=8 << 20,
    )
    parts = lax.all_to_all(partial, SEQ_AXES, 0, 0, tiled=False)

    own = lax.dynamic_index_in_dim(wg[:, 128:].reshape(NZ, 8, NZ, LOCAL), iz, 2, keepdims=False)
    out_cols = lax.all_gather(own, SEQ_AXES, axis=0, tiled=False)
    out_cols = out_cols.transpose(1, 0, 2, 3).reshape(NZ, 2 * HD, LOCAL)
    w_dec_t = wg[:, 64:128].transpose(1, 0, 2).reshape(64, WIDTH)
    w2_t = nt_dot(w_dec_t, w_out).astype(bf16)
    parts, out_cols, w2_t = lax.optimization_barrier((parts, out_cols, w2_t))

    att, dec_own = call(
        combine_kernel, "combine",
        [((ROWS + 64, 2 * HD), bf16), ((ROWS, 64), f32)], [VMEM, VMEM], (parts, w2_t),
        scratch=[pltpu.VMEM((ROWS, 2 * HD), f32)], mib=32,
    )
    hid_out = [((ROWS, LOCAL), f32), ((ROWS, 64), f32)]

    def cols_scratch(count):
        return [
            pltpu.VMEM((count, 2 * HD, LOCAL), bf16), pltpu.SemaphoreType.DMA((count,)),
        ]

    def project(shifts, chunks, hid, pred):
        return call(
            functools.partial(middle_kernel, shifts), "middle", hid_out,
            [SMEM] + [VMEM] * 2 + [ANY] + [VMEM] * 2,
            (scalars, *chunks, out_cols, hid, pred),
            scratch=cols_scratch(2), flops=2 * 2 * ROWS * 256 * LOCAL, nbytes=4 << 20,
        )

    up1, down1 = ring_step(att, att)
    up2, down2 = ring_step(up1, down1)
    hid, pred, own_noise = call(
        start_kernel, "start", hid_out + [((ROWS, 64), f32)],
        [SMEM, SMEM] + [VMEM] * 3 + [ANY] + [VMEM] * 5,
        (
            scalars, flags, att, up1, down1, out_cols, parts[:, 9], text_embed, w_patch,
            own_times, dec_own,
        ),
        scratch=cols_scratch(3), flops=3 * 2 * ROWS * 256 * LOCAL, nbytes=4 << 20,
    )
    up2, down2, hid, pred = lax.optimization_barrier((up2, down2, hid, pred))
    up3, down3 = ring_step(up2, down2)
    hid, pred = project((2, -2), (up2, down2), hid, pred)
    up3, down3, hid, pred = lax.optimization_barrier((up3, down3, hid, pred))
    far = ring_end(up3, down3)
    hid, pred = project((3, -3), (up3, down3), hid, pred)
    hidden_out, predicted, error = call(
        close_kernel, "close",
        [((ROWS, LOCAL), bf16), ((ROWS, 64), f32), ((1, ROWS), f32)],
        [SMEM, SMEM] + [VMEM] * 2 + [ANY] + [VMEM] * 3,
        (scalars, flags, *far, out_cols, hid, pred, own_noise),
        scratch=[pltpu.VMEM((ROWS, LOCAL), f32)] + cols_scratch(1),
    )
    return hidden_out, predicted, error.reshape(ROWS)


def solution(mesh):
    fine = Mesh(mesh.devices.reshape(4, 4, 2, NZ), ("x", "y", "c", "z"))
    seq, tp = SEQ_AXES, "z"
    in_specs = (
        P(seq, tp),
        P(seq, None, None),
        P(seq, None, None),
        P(seq),
        P(),
        P(),
        P(),
        P(None, tp),
        P(None, tp),
        P(None, None, tp),
        P(tp, None),
        P(tp, None),
    )
    out_specs = (P(seq, tp), P(seq, None), P(seq))
    return jax.shard_map(
        per_device, mesh=fine, in_specs=in_specs, out_specs=out_specs, check_vma=False
    )
```

```python
import functools
import math

import jax
import jax.numpy as jnp
from jax import lax
from jax.experimental import pallas as pl
from jax.experimental.pallas import tpu as pltpu
from jax.sharding import Mesh, PartitionSpec as P

HD = 128
TSTEPS = 1000
EPS = 1e-05
PATCH_ROWS = 256
BLOCKS = 64
IMAGES = 32
TEXTS = BLOCKS - IMAGES
STRIPES = 32
SROWS = 8
NZ = 8
WIDTH = 4096
LOCAL = WIDTH // NZ
S = BLOCKS * PATCH_ROWS
DOCS = 4
SEQ_AXES = ("x", "y", "c")
MASKED = -1e30
FLOOR = -1e29
SCALE2 = math.log2(math.e) / math.sqrt(HD)
QB = 16
KB = 16
TEXT_ROWS = TEXTS * SROWS
ROWS = BLOCKS * SROWS
VMEM = pl.BlockSpec(memory_space=pltpu.VMEM)
SMEM = pl.BlockSpec(memory_space=pltpu.SMEM)
ANY = pl.BlockSpec(memory_space=pl.ANY)
HBM = pl.BlockSpec(memory_space=pltpu.HBM)


def shifted(a, axis, shift):
    count = lax.axis_size(axis)
    return lax.ppermute(a, axis, [(i, (i + shift) % count) for i in range(count)])


def ring_pair(up, down):
    return shifted(up, "z", 1), shifted(down, "z", -1)


def ring_far(up, down):
    half = up.shape[0] // 2
    return shifted(up[:half], "z", 1), shifted(down[half:], "z", -1)


def nt_dot(a, b):
    return lax.dot_general(a, b, (((1,), (1,)), ((), ())), preferred_element_type=jnp.float32)


def pack_kernel(
    sc_ref, coef_ref, text_ref, clean_ref, noise_ref, feat_ref, wp_ref, wd_ref,
    out_ref, packed_ref,
):
    @pl.when(sc_ref[2] == 0)
    def _():
        packed_ref[...] = wp_ref[...]

    @pl.when(sc_ref[2] == 1)
    def _():
        packed_ref[...] = wd_ref[...]

    noise = noise_ref[...].astype(jnp.float32)
    noised = coef_ref[0] * clean_ref[...].astype(jnp.float32) + coef_ref[1] * noise
    pairs = jnp.transpose(jnp.concatenate([noised, noise], axis=0))
    feats = jnp.concatenate(
        [feat_ref[0:1, :HD], feat_ref[0:1, HD:], jnp.zeros((6, HD), jnp.float32)], axis=0
    )
    for s in range(0, STRIPES, 2):
        rows = [
            text_ref[b * PATCH_ROWS + s * SROWS : b * PATCH_ROWS + (s + 2) * SROWS, :].astype(
                jnp.float32
            )
            for b in range(2)
        ]
        for n in range(2):
            at = n * SROWS
            out_ref[s + n, :, :LOCAL] = jnp.concatenate(
                [rows[0][at : at + SROWS], rows[1][at : at + SROWS]], axis=0
            ).astype(jnp.bfloat16)
            patch = pairs[(s + n) * SROWS : (s + n + 1) * SROWS]
            out_ref[s + n, :, LOCAL:] = jnp.concatenate([patch, feats], axis=0).astype(jnp.bfloat16)


def sort_kernel(
    sc_ref, image_ref, doc_ref, got_ref, wt_ref,
    pay_ref, noised_ref, back_ref, times_ref, slot_ref, flag_ref, start_ref, text_ref, both_ref,
):
    seq = sc_ref[4]

    def clear(b, carry):
        flag_ref[b] = 0
        slot_ref[b] = 0
        return carry

    lax.fori_loop(0, BLOCKS, clear, 0)

    def mark(i, carry):
        block = image_ref[i]
        flag_ref[block] = 1
        slot_ref[block] = TEXTS + i
        return carry

    lax.fori_loop(0, IMAGES, mark, 0)
    docs = doc_ref[...]
    for d in range(DOCS):
        start_ref[d] = jnp.sum((docs < d).astype(jnp.int32))

    feats = jnp.concatenate(
        [got_ref[i, :, LOCAL:].astype(jnp.float32)[8:10].reshape(1, 2, HD) for i in range(IMAGES)],
        axis=0,
    )
    first, second = feats[:, 0, :].astype(jnp.bfloat16), feats[:, 1, :].astype(jnp.bfloat16)
    times = jnp.dot(first, wt_ref[:HD], preferred_element_type=jnp.float32) + jnp.dot(
        second, wt_ref[HD:], preferred_element_type=jnp.float32
    )
    both_ref[...] = times
    for n in range(2):
        image = jnp.maximum(slot_ref[2 * seq + n] - TEXTS, 0)
        times_ref[n : n + 1, :] = both_ref[pl.ds(image, 1), :]
    pay_ref[TEXT_ROWS:, :] = times.astype(jnp.bfloat16)

    def place(pair, rank):
        wide = got_ref[pair, :, :LOCAL].astype(jnp.float32)
        for n in range(2):
            b = 2 * pair + n
            is_text = flag_ref[b] == 0

            @pl.when(is_text)
            def _(b=b, n=n, rank=rank):
                slot_ref[b] = rank
                text_ref[pl.ds(pl.multiple_of(rank * SROWS, SROWS), SROWS), :] = wide[
                    n * SROWS : (n + 1) * SROWS
                ]

            rank = rank + jnp.where(is_text, 1, 0)
        return rank

    lax.fori_loop(0, BLOCKS // 2, place, 0)
    pay_ref[:TEXT_ROWS, :] = text_ref[...].astype(jnp.bfloat16)

    for i in range(0, IMAGES, 2):
        pair = jnp.concatenate(
            [got_ref[i + n, :, LOCAL:].astype(jnp.float32)[:SROWS] for n in range(2)], axis=0
        )
        noised_ref[i * SROWS : (i + 2) * SROWS, :] = pair[:, :64].astype(jnp.bfloat16)

    def back(pair, carry):
        parts = [
            got_ref[jnp.maximum(slot_ref[2 * pair + n] - TEXTS, 0), :, LOCAL:].astype(jnp.float32)[
                :SROWS
            ]
            for n in range(2)
        ]
        back_ref[pair] = jnp.concatenate(parts, axis=0).astype(jnp.bfloat16)
        return carry

    lax.fori_loop(0, BLOCKS // 2, back, 0)


def fold_chunks(
    z, shifts, chunks, w_hbm, wg_hbm, gain_ref, noised_ref, w_ref, wg_ref, sems,
    acc_ref, sq_ref, dec_ref,
):
    sources = [lax.rem(z - shift + NZ, NZ) for shift in shifts]
    copies = [
        (
            pltpu.make_async_copy(wg_hbm.at[:, src], wg_ref.at[n], sems.at[0, n]),
            pltpu.make_async_copy(w_hbm.at[:, src], w_ref.at[n], sems.at[1, n]),
        )
        for n, src in enumerate(sources)
    ]
    for pair in copies:
        pair[0].start()
        pair[1].start()
    for n, (src, block) in enumerate(zip(sources, chunks)):
        times = block[TEXT_ROWS:].astype(jnp.float32)
        copies[n][0].wait()
        patch = jnp.dot(noised_ref[...], wg_ref[n, 0], preferred_element_type=jnp.float32)
        timed = jnp.broadcast_to(times[:, None, :], (IMAGES, SROWS, LOCAL))
        image = (patch + timed.reshape(IMAGES * SROWS, LOCAL)).astype(jnp.bfloat16)
        both = jnp.concatenate([block[:TEXT_ROWS], image], axis=0)
        wide = both.astype(jnp.float32)
        square = wide * wide
        sq_ref[...] += sum(square[:, g * HD : (g + 1) * HD] for g in range(LOCAL // HD))
        dec_ref[...] += nt_dot(both, wg_ref[n, 1])
        left = (wide * gain_ref[src]).astype(jnp.bfloat16)
        copies[n][1].wait()
        for j in range(3):
            acc_ref[j] += jnp.dot(left, w_ref[n, j], preferred_element_type=jnp.float32)


def part_kernel(shifts, first, sc_ref, *refs):
    n = len(shifts)
    chunks, refs = refs[:n], refs[n:]
    w_hbm, wg_hbm, gain_ref, noised_ref = refs[:4]
    refs = refs[4:]
    moves = []
    if first:
        out_hbm, acc_ref, sq_ref, dec_ref, cut_hbm, w_ref, wg_ref, sems, cut_sems = refs
        rows = pl.ds(pl.multiple_of(sc_ref[2] * HD, HD), HD)
        for d in range(NZ):
            source = out_hbm.at[rows, d * LOCAL : (d + 1) * LOCAL]
            moves.append(pltpu.make_async_copy(source, cut_hbm.at[d], cut_sems.at[d]))
            moves[d].start()
        acc_ref[...] = jnp.zeros(acc_ref.shape, jnp.float32)
        sq_ref[...] = jnp.zeros(sq_ref.shape, jnp.float32)
        dec_ref[...] = jnp.zeros(dec_ref.shape, jnp.float32)
    else:
        acc_in, sq_in, dec_in, acc_ref, sq_ref, dec_ref, w_ref, wg_ref, sems = refs
        acc_ref[...] = acc_in[...]
        sq_ref[...] = sq_in[...]
        dec_ref[...] = dec_in[...]
    fold_chunks(
        sc_ref[3], shifts, [c[...] for c in chunks], w_hbm, wg_hbm, gain_ref, noised_ref,
        w_ref, wg_ref, sems, acc_ref, sq_ref, dec_ref,
    )
    for move in moves:
        move.wait()


def finish_kernel(
    sc_ref, slot_ref, f0, f1, w_hbm, wg_hbm, gain_ref, noised_ref, acc_in, sq_in, dec_in,
    my_q, my_kv, their_q, their_kv, dec_out,
    acc_ref, sq_ref, dec_ref, w_ref, wg_ref, sems, six_ref,
):
    c = sc_ref[2]
    acc_ref[...] = acc_in[...]
    sq_ref[...] = sq_in[...]
    dec_ref[...] = dec_in[...]
    fold_chunks(
        sc_ref[3], (4,), [jnp.concatenate([f0[...], f1[...]], axis=0)], w_hbm, wg_hbm, gain_ref, noised_ref,
        w_ref, wg_ref, sems, acc_ref, sq_ref, dec_ref,
    )
    squares = jnp.sum(sq_ref[...], axis=1, keepdims=True)
    inverse = lax.rsqrt(squares * (1.0 / WIDTH) + EPS)
    for j in range(3):
        scale = inverse * SCALE2 if j == 0 else inverse
        for h in range(2):
            six_ref[2 * j + h] = acc_ref[j, :, h * HD : (h + 1) * HD] * scale

    def arrange(pair, carry):
        first = pl.multiple_of(slot_ref[2 * pair] * SROWS, SROWS)
        second = pl.multiple_of(slot_ref[2 * pair + 1] * SROWS, SROWS)
        at = pl.ds(pl.multiple_of(pair * 2 * SROWS, 2 * SROWS), 2 * SROWS)

        def rows_of(index):
            return jnp.concatenate(
                [six_ref[index, pl.ds(first, SROWS), :], six_ref[index, pl.ds(second, SROWS), :]],
                axis=0,
            ).astype(jnp.bfloat16)

        for q_ref, kv_ref, head in ((my_q, my_kv, c), (their_q, their_kv, 1 - c)):
            q_ref[at, :] = rows_of(head)
            kv_ref[0, at, :] = rows_of(2 + head)
            kv_ref[1, at, :] = rows_of(4 + head)
        dec_out[pair] = jnp.concatenate(
            [dec_ref[pl.ds(first, SROWS), :], dec_ref[pl.ds(second, SROWS), :]], axis=1
        )
        return carry

    lax.fori_loop(0, BLOCKS // 2, arrange, 0)


def attend_kernel(
    sc_ref, start_ref, flag_ref, q0, q1, q2, q3, kv0, kv1, kv3, k2, v2, dec_ref, img_ref,
    out_ref, qs, ks, vs, vx, m_ref, acc_ref, low_ref, high_ref, s_even, s_odd, t_even, t_odd, sems,
):
    x, y, c = sc_ref[0], sc_ref[1], sc_ref[2]
    copies = []

    def bring(source, target):
        copy = pltpu.make_async_copy(source, target, sems.at[len(copies)])
        copy.start()
        copies.append(copy)

    for i in range(2):
        cc = c if i == 0 else 1 - c
        for ref, shift in ((kv0, 0), (kv1, 1), (kv3, 3)):
            at = lax.rem(x - shift + 4, 4) * 2 + cc
            bring(ref.at[i, 1], vs.at[at])
            bring(ref.at[i, 0], ks.at[at])
        at = lax.rem(x + 2, 4) * 2 + cc
        bring(v2.at[i], vs.at[at])
        bring(k2.at[i], ks.at[at])
        for ref, shift in ((q0, 0), (q1, 1), (q2, 2), (q3, 3)):
            bring(ref.at[i], qs.at[:, lax.rem(y - shift + 4, 4) * 2 + cc])

    rows = QB * 64
    cols = KB * 64
    span = QB * PATCH_ROWS
    dests = QB // 2
    tiles = BLOCKS // QB
    starts = [start_ref[d] for d in range(DOCS)]
    for i in range(tiles):
        rho = lax.broadcasted_iota(jnp.int32, (8, rows), 1)
        blk = 2 * (rho >> 7) + ((rho >> 3) & 1)
        first = (QB * i + blk) * PATCH_ROWS
        q_pos = first + 64 * x + 8 * ((rho >> 4) & 7) + (rho & 7)
        low = jnp.zeros((8, rows), jnp.int32)
        high_doc = jnp.full((8, rows), S - 1, jnp.int32)
        for start in starts:
            low = jnp.where(start <= q_pos, jnp.maximum(low, start), low)
            high_doc = jnp.where(start > q_pos, jnp.minimum(high_doc, start - 1), high_doc)
        flag = jnp.zeros((8, rows), jnp.int32)
        for n in range(QB):
            flag = jnp.where(blk == n, flag_ref[QB * i + n], flag)
        low_ref[i] = low
        high_ref[i] = jnp.where(flag == 1, jnp.minimum(high_doc, first + PATCH_ROWS - 1), q_pos)
    acc_ref[...] = jnp.zeros((HD + 16, rows), jnp.float32)
    m_ref[...] = jnp.zeros((8, rows), jnp.float32)
    for copy in copies:
        copy.wait()
    for p in range(8):
        vx[p, :HD, :] = jnp.transpose(vs[p].astype(jnp.float32)).astype(jnp.bfloat16)
        vx[p, HD:, :] = jnp.ones((16, ROWS), jnp.bfloat16)

    score_refs, top_refs = (s_even, s_odd), (t_even, t_odd)
    count = tiles * (tiles + 1) // 2

    def tile_of(t):
        i = sum((t >= n * (n + 1) // 2).astype(jnp.int32) for n in range(1, tiles))
        return i, t - (i * (i + 1)) // 2

    def keys_at(j):
        return pl.ds(pl.multiple_of(j * KB * SROWS, KB * SROWS), KB * SROWS)

    def score(t, slot, masked):
        i, j = tile_of(t)
        k = ks[:, keys_at(j), :].reshape(cols, HD)
        s = nt_dot(k, qs[pl.ds(i * dests, dests)].reshape(rows, HD))
        if masked:
            kappa = lax.broadcasted_iota(jnp.int32, (cols, 1), 0)
            k_pos = (
                (KB * j + ((kappa >> 3) & 15)) * PATCH_ROWS
                + 64 * (kappa >> 8) + 16 * y + 8 * ((kappa >> 7) & 1) + (kappa & 7)
            )
            seen = jnp.logical_and(k_pos >= low_ref[i, 0:1], k_pos <= high_ref[i, 0:1])
            s = jnp.where(seen, s, MASKED)
        score_refs[slot][...] = s
        top_refs[slot][0:1] = jnp.max(s, axis=0, keepdims=True)

    def weigh(t, slot):
        i, j = tile_of(t)
        v = jnp.concatenate([vx[p, :, keys_at(j)] for p in range(8)], axis=1)
        m_old = jnp.where(j == 0, FLOOR, m_ref[0:1])
        m_new = jnp.maximum(m_old, top_refs[slot][0:1])
        m_ref[0:1] = m_new
        alpha = jnp.where(j == 0, 0.0, jnp.exp2(m_old - m_new))
        p = jnp.exp2(score_refs[slot][...] - m_new).astype(jnp.bfloat16)
        acc_ref[...] = acc_ref[...] * alpha + jnp.dot(v, p, preferred_element_type=jnp.float32)

    def emit(t):
        i, j = tile_of(t)

        @pl.when(i == j)
        def _():
            total = acc_ref[HD : HD + 1]
            some = total > 0.0
            safe = jnp.where(some, total, 1.0)
            o = jnp.transpose(acc_ref[:HD] / safe).astype(jnp.bfloat16)
            level = jnp.where(some, m_ref[0:1] + jnp.log2(safe), MASKED)
            high_part = level.astype(jnp.bfloat16).astype(jnp.float32)
            rest = level - high_part
            mid_part = rest.astype(jnp.bfloat16).astype(jnp.float32)
            low_part = rest - mid_part
            head = jnp.concatenate(
                [high_part, mid_part, low_part, jnp.zeros((5, rows), jnp.float32)], axis=0
            )
            for d in range(dests):
                dest = dests * i + d
                out_ref[dest, 0:8] = o[HD * d : HD * (d + 1)].reshape(8, 16, HD)
                out_ref[dest, 8] = jnp.concatenate(
                    [head[:, HD * d : HD * (d + 1)], dec_ref[dest]], axis=0
                ).astype(jnp.bfloat16)
                out_ref[dest, 9] = img_ref[dest]

    def advance(t, slot):
        i, j = tile_of(t + 1)
        last = i * span + span - 1
        low_last = 0
        for start in starts:
            low_last = jnp.where(start <= last, jnp.maximum(start, low_last), low_last)
        full = jnp.logical_and(j < i, low_last <= j * span)

        @pl.when(full)
        def _():
            score(t + 1, 1 - slot, False)
            weigh(t, slot)

        @pl.when(jnp.logical_not(full))
        def _():
            score(t + 1, 1 - slot, True)
            weigh(t, slot)

        emit(t)

    def two(u, carry):
        advance(2 * u, 0)
        advance(2 * u + 1, 1)
        return carry

    score(jnp.int32(0), 0, True)
    lax.fori_loop(0, (count - 2) // 2, two, 0)
    advance(jnp.int32(count - 2), 0)
    weigh(jnp.int32(count - 1), 1)
    emit(jnp.int32(count - 1))


def combine_kernel(in_ref, w2_ref, att_ref, dec_ref, full_ref):
    for x in range(4):
        for c in range(2):
            heads = [in_ref[x * 8 + y * 2 + c, 8].astype(jnp.float32) for y in range(4)]
            levels = [h[0:1] + h[1:2] + h[2:3] for h in heads]
            top = functools.reduce(jnp.maximum, levels)
            weights = [jnp.exp2(level - top) for level in levels]
            total = functools.reduce(jnp.add, weights)
            part = None
            for y in range(4):
                share = jnp.transpose(jnp.broadcast_to(weights[y] / total, (HD, HD)))
                o = in_ref[x * 8 + y * 2 + c, 0:8].reshape(HD, HD).astype(jnp.float32)
                part = o * share if part is None else part + o * share
            for p in range(8):
                for b in range(2):
                    full_ref[
                        b * PATCH_ROWS + 64 * x + 8 * p : b * PATCH_ROWS + 64 * x + 8 * p + 8,
                        c * HD : (c + 1) * HD,
                    ] = part[(2 * p + b) * 8 : (2 * p + b) * 8 + 8]
            for y in range(4):
                stripe = x * 8 + y * 2 + c
                for b in range(2):
                    at = b * PATCH_ROWS + stripe * SROWS
                    dec_ref[at : at + SROWS, :] = heads[y][8:16, b * 64 : (b + 1) * 64]
    att_ref[:ROWS, :] = full_ref[...].astype(jnp.bfloat16)
    att_ref[ROWS:, :] = w2_ref[...]


def project_chunks(sc_ref, shifts, chunks, mine_hbm, theirs_hbm, cols_ref, sems, hid_ref, pred_ref):
    c, z = sc_ref[2], sc_ref[3]
    copies = []
    for n, shift in enumerate(shifts):
        src = lax.rem(z - shift + NZ, NZ)
        for m, (hbm, half) in enumerate(((mine_hbm, c), (theirs_hbm, 1 - c))):
            rows = pl.ds(pl.multiple_of(half * HD, HD), HD)
            copies.append(
                pltpu.make_async_copy(hbm.at[src], cols_ref.at[n, rows], sems.at[m, n])
            )
            copies[-1].start()
    for n, block in enumerate(chunks):
        attended = block[:ROWS]
        pred_ref[...] += nt_dot(attended, block[ROWS:])
        copies[2 * n].wait()
        copies[2 * n + 1].wait()
        hid_ref[...] += jnp.dot(attended, cols_ref[n], preferred_element_type=jnp.float32)


def start_kernel(
    sc_ref, flag_ref, c0, c1, c2, mine_hbm, theirs_hbm, parts_ref, text_ref, wp_ref, times_ref, dec_ref,
    hid_ref, pred_ref, noise_ref, cols_ref, sems,
):
    seq = sc_ref[4]
    for b in range(2):
        at = slice(b * PATCH_ROWS, (b + 1) * PATCH_ROWS)
        pairs = parts_ref[...].astype(jnp.float32)[:, b * SROWS : (b + 1) * SROWS].reshape(
            PATCH_ROWS, 2 * 64
        )
        noise_ref[at, :] = pairs[:, 64:]
        patch = jnp.dot(
            pairs[:, :64].astype(jnp.bfloat16), wp_ref[...], preferred_element_type=jnp.float32
        )
        image = (patch + times_ref[b : b + 1, :]).astype(jnp.bfloat16).astype(jnp.float32)
        text = text_ref[at, :].astype(jnp.float32)
        hid_ref[at, :] = jnp.where(flag_ref[2 * seq + b] == 1, image, text)
    pred_ref[...] = dec_ref[...]
    project_chunks(
        sc_ref, (0, 1, -1), [c0[...], c1[...], c2[...]], mine_hbm, theirs_hbm, cols_ref, sems,
        hid_ref, pred_ref,
    )


def middle_kernel(
    shifts, sc_ref, c0, c1, mine_hbm, theirs_hbm, hid_in, pred_in, hid_ref, pred_ref, cols_ref, sems
):
    hid_ref[...] = hid_in[...]
    pred_ref[...] = pred_in[...]
    project_chunks(
        sc_ref, shifts, [c0[...], c1[...]], mine_hbm, theirs_hbm, cols_ref, sems,
        hid_ref, pred_ref,
    )


def close_kernel(
    sc_ref, flag_ref, f0, f1, mine_hbm, theirs_hbm, hid_in, pred_in, noise_ref,
    out_ref, pred_t_ref, err_ref, hid_ref, pred_ref, cols_ref, sems,
):
    seq = sc_ref[4]
    hid_ref[...] = hid_in[...]
    pred_ref[...] = pred_in[...]
    project_chunks(
        sc_ref, (4,), [jnp.concatenate([f0[...], f1[...]], axis=0)], mine_hbm, theirs_hbm, cols_ref, sems, hid_ref, pred_ref
    )
    out_ref[...] = hid_ref[...].astype(jnp.bfloat16)
    pred_t_ref[...] = jnp.transpose(pred_ref[...])
    gap = pred_ref[...] - noise_ref[...]
    square = jnp.transpose(gap * gap)
    mean = jnp.sum(square, axis=0, keepdims=True) * (1.0 / 64)
    for b in range(2):
        at = slice(b * PATCH_ROWS, (b + 1) * PATCH_ROWS)
        err_ref[0:1, at] = jnp.where(flag_ref[2 * seq + b] == 1, mean[:, at], 0.0)


def kernel_params(mib):
    return pltpu.CompilerParams(vmem_limit_bytes=mib * 1024 * 1024)


def call(kernel, name, outs, in_specs, args, scratch=(), mib=24, flops=0, nbytes=0, out_specs=None):
    return pl.pallas_call(
        kernel,
        out_shape=tuple(jax.ShapeDtypeStruct(shape, dtype) for shape, dtype in outs),
        in_specs=in_specs,
        out_specs=out_specs or tuple(VMEM for _ in outs),
        scratch_shapes=list(scratch),
        compiler_params=kernel_params(mib),
        cost_estimate=pl.CostEstimate(flops=flops, bytes_accessed=nbytes, transcendentals=0),
        name=name,
    )(*args)


def per_device(
    text_embed, latents, noise, timesteps, image_block, doc_ids, norm_gain,
    w_patch, w_time, w_qkv, w_out, w_dec,
):
    ix, iy, ic, iz = (lax.axis_index(a) for a in ("x", "y", "c", "z"))
    seq = ix * 8 + iy * 2 + ic
    f32, bf16, i32 = jnp.float32, jnp.bfloat16, jnp.int32
    scalars = jnp.stack([ix, iy, ic, iz, seq]).astype(i32)

    step = timesteps.astype(f32)
    signal = jnp.cos((step / TSTEPS + 0.008) / 1.008 * (math.pi / 2)) ** 2
    coefs = jnp.concatenate([jnp.sqrt(signal), jnp.sqrt(1.0 - signal)])
    freq_count = w_time.shape[0] // 2
    freqs = jnp.exp(-math.log(10000.0) * jnp.arange(freq_count, dtype=f32) / freq_count)
    angles = step[:, None] * freqs[None, :]
    feats = jnp.concatenate([jnp.cos(angles), jnp.sin(angles)], axis=1)
    sent, packed = call(
        pack_kernel, "pack",
        [((STRIPES, 2 * SROWS, LOCAL + HD), bf16), ((64, LOCAL), bf16)], [SMEM] * 2 + [VMEM] * 6,
        (scalars, coefs, text_embed, latents[0].T, noise[0].T, feats, w_patch, w_dec.T), mib=60,
    )
    got = lax.all_to_all(sent, SEQ_AXES, 0, 0, tiled=False)
    wg = lax.all_gather(packed, ("c", "z"), axis=0, tiled=False).reshape(2, NZ, 64, LOCAL)

    payload, noised, image_back, own_times, slots, flags, starts = call(
        sort_kernel, "sort",
        [
            ((TEXT_ROWS + IMAGES, LOCAL), bf16),
            ((IMAGES * SROWS, 64), bf16),
            ((STRIPES, 2 * SROWS, HD), bf16),
            ((2, LOCAL), f32),
            ((BLOCKS,), i32),
            ((BLOCKS,), i32),
            ((DOCS,), i32),
        ],
        [SMEM, SMEM, VMEM, VMEM, VMEM],
        (scalars, image_block, doc_ids.reshape(128, 128), got, w_time),
        scratch=[pltpu.VMEM((TEXT_ROWS, LOCAL), f32), pltpu.VMEM((IMAGES, LOCAL), f32)],
        mib=16, out_specs=(VMEM,) * 4 + (SMEM,) * 3,
    )
    w_cols = w_qkv.transpose(1, 0, 2).reshape(3, NZ, LOCAL, 2 * HD)
    gains = norm_gain.reshape(NZ, 1, LOCAL)
    sums = [((3, ROWS, 2 * HD), f32), ((ROWS, HD), f32), ((ROWS, 64), f32)]

    def fold(shifts, chunks, state):
        count = len(shifts)
        scratch = [
            pltpu.VMEM((count, 3, LOCAL, 2 * HD), bf16),
            pltpu.VMEM((count, 2, 64, LOCAL), bf16),
            pltpu.SemaphoreType.DMA((2, count)),
        ]
        cost = {"flops": count * 2 * ROWS * LOCAL * 6 * HD, "nbytes": 4 << 20}
        kernel = functools.partial(part_kernel, shifts, not state)
        specs = [SMEM] + [VMEM] * count + [HBM] * 2 + [VMEM] * 2
        given = (scalars, *chunks, w_cols, wg, gains, noised)
        if state:
            return call(
                kernel, "part", sums, specs + [VMEM] * 3, (*given, *state), scratch=scratch, **cost
            )
        return call(
            kernel, "part", sums + [((NZ, HD, LOCAL), bf16)], specs + [HBM], (*given, w_out),
            scratch=scratch + [pltpu.SemaphoreType.DMA((NZ,))],
            **cost,
        )

    up1, down1 = ring_pair(payload, payload)
    up2, down2 = ring_pair(up1, down1)
    *state, out_rows = fold((0, 1, -1), (payload, up1, down1), ())
    up2, down2, *state = lax.optimization_barrier((up2, down2, *state))
    up3, down3 = ring_pair(up2, down2)
    state = fold((2, -2), (up2, down2), state)
    up3, down3, out_rows, *state = lax.optimization_barrier((up3, down3, out_rows, *state))
    far = ring_far(up3, down3)
    cols_mine = lax.all_to_all(out_rows, "z", 0, 0, tiled=False)
    state = fold((3, -3), (up3, down3), state)
    my_q, my_kv, their_q, their_kv, dec_rows = call(
        finish_kernel, "finish",
        [
            ((ROWS, HD), bf16),
            ((2, ROWS, HD), bf16),
            ((ROWS, HD), bf16),
            ((2, ROWS, HD), bf16),
            ((STRIPES, SROWS, HD), f32),
        ],
        [SMEM, SMEM, VMEM, VMEM, HBM, HBM] + [VMEM] * 5,
        (scalars, slots, *far, w_cols, wg, gains, noised, *state),
        scratch=[
            pltpu.VMEM((3, ROWS, 2 * HD), f32),
            pltpu.VMEM((ROWS, HD), f32),
            pltpu.VMEM((ROWS, 64), f32),
            pltpu.VMEM((1, 3, LOCAL, 2 * HD), bf16),
            pltpu.VMEM((1, 2, 64, LOCAL), bf16),
            pltpu.SemaphoreType.DMA((2, 1)),
            pltpu.VMEM((6, ROWS, HD), f32),
        ],
    )

    got_q = lax.ppermute(their_q, "c", [(0, 1), (1, 0)])
    got_kv = lax.ppermute(their_kv, "c", [(0, 1), (1, 0)])
    q = jnp.stack([my_q, got_q])
    kv = jnp.stack([my_kv, got_kv])
    kv1, kv3 = shifted(kv, "x", 1), shifted(kv, "x", -1)
    q1, q3 = shifted(q, "y", 1), shifted(q, "y", -1)
    k2, v2 = shifted(kv1[:, 0], "x", 1), shifted(kv3[:, 1], "x", -1)
    q2 = shifted(q, "y", 2)
    by_dest = [a.reshape(2, STRIPES, 16, HD) for a in (q, q1, q2, q3)]

    (partial,) = call(
        attend_kernel, "attend", [((STRIPES, 10, 16, HD), bf16)],
        [SMEM] * 3 + [ANY] * 9 + [VMEM] * 2,
        (scalars, starts, flags, *by_dest, kv, kv1, kv3, k2, v2, dec_rows, image_back),
        scratch=[
            pltpu.VMEM((STRIPES, 8, 16, HD), bf16),
            pltpu.VMEM((8, ROWS, HD), bf16),
            pltpu.VMEM((8, ROWS, HD), bf16),
            pltpu.VMEM((8, HD + 16, ROWS), bf16),
            pltpu.VMEM((8, QB * 64), f32),
            pltpu.VMEM((HD + 16, QB * 64), f32),
            pltpu.VMEM((BLOCKS // QB, 8, QB * 64), i32),
            pltpu.VMEM((BLOCKS // QB, 8, QB * 64), i32),
            pltpu.VMEM((KB * 64, QB * 64), f32),
            pltpu.VMEM((KB * 64, QB * 64), f32),
            pltpu.VMEM((8, QB * 64), f32),
            pltpu.VMEM((8, QB * 64), f32),
            pltpu.SemaphoreType.DMA((24,)),
        ],
        mib=32, flops=5 << 30, nbytes=8 << 20,
    )
    partial, cols_mine = lax.optimization_barrier((partial, cols_mine))
    cols_theirs = lax.ppermute(cols_mine, "c", [(0, 1), (1, 0)])
    parts = lax.all_to_all(partial, SEQ_AXES, 0, 0, tiled=False)

    w_dec_t = wg[1].transpose(1, 0, 2).reshape(64, WIDTH)
    w2_t = nt_dot(w_dec_t, w_out).astype(bf16)

    att, dec_own = call(
        combine_kernel, "combine",
        [((ROWS + 64, 2 * HD), bf16), ((ROWS, 64), f32)], [VMEM, VMEM], (parts, w2_t),
        scratch=[pltpu.VMEM((ROWS, 2 * HD), f32)],
    )
    hid_out = [((ROWS, LOCAL), f32), ((ROWS, 64), f32)]

    def cols_scratch(count):
        return [
            pltpu.VMEM((count, 2 * HD, LOCAL), bf16), pltpu.SemaphoreType.DMA((2, count)),
        ]

    def project(shifts, chunks, hid, pred):
        return call(
            functools.partial(middle_kernel, shifts), "middle", hid_out,
            [SMEM] + [VMEM] * 2 + [ANY] * 2 + [VMEM] * 2,
            (scalars, *chunks, cols_mine, cols_theirs, hid, pred),
            scratch=cols_scratch(2), flops=2 * 2 * ROWS * 256 * LOCAL, nbytes=4 << 20,
        )

    up1, down1 = ring_pair(att, att)
    up2, down2 = ring_pair(up1, down1)
    hid, pred, own_noise = call(
        start_kernel, "start", hid_out + [((ROWS, 64), f32)],
        [SMEM, SMEM] + [VMEM] * 3 + [ANY] * 2 + [VMEM] * 5,
        (
            scalars, flags, att, up1, down1, cols_mine, cols_theirs, parts[:, 9], text_embed, w_patch,
            own_times, dec_own,
        ),
        scratch=cols_scratch(3), flops=3 * 2 * ROWS * 256 * LOCAL, nbytes=4 << 20,
    )
    up2, down2, hid, pred = lax.optimization_barrier((up2, down2, hid, pred))
    up3, down3 = ring_pair(up2, down2)
    hid, pred = project((2, -2), (up2, down2), hid, pred)
    up3, down3, hid, pred = lax.optimization_barrier((up3, down3, hid, pred))
    far = ring_far(up3, down3)
    hid, pred = project((3, -3), (up3, down3), hid, pred)
    hidden_out, predicted_t, error = call(
        close_kernel, "close",
        [((ROWS, LOCAL), bf16), ((64, ROWS), f32), ((1, ROWS), f32)],
        [SMEM, SMEM] + [VMEM] * 2 + [ANY] * 2 + [VMEM] * 3,
        (scalars, flags, *far, cols_mine, cols_theirs, hid, pred, own_noise),
        scratch=[pltpu.VMEM((ROWS, LOCAL), f32), pltpu.VMEM((ROWS, 64), f32)] + cols_scratch(1),
    )
    return hidden_out, predicted_t.T, error.reshape(ROWS)


def solution(mesh):
    fine = Mesh(mesh.devices.reshape(4, 4, 2, NZ), ("x", "y", "c", "z"))
    seq, tp = SEQ_AXES, "z"
    in_specs = (
        P(seq, tp),
        P(seq, None, None),
        P(seq, None, None),
        P(seq),
        P(),
        P(),
        P(),
        P(None, tp),
        P(None, tp),
        P(None, None, tp),
        P(tp, None),
        P(tp, None),
    )
    out_specs = (P(seq, tp), P(seq, None), P(seq))
    return jax.shard_map(
        per_device, mesh=fine, in_specs=in_specs, out_specs=out_specs, check_vma=False
    )
```

```python
import functools
import math

import jax
import jax.numpy as jnp
from jax import lax
from jax.experimental import pallas as pl
from jax.experimental.pallas import tpu as pltpu
from jax.sharding import Mesh, PartitionSpec as P

HD = 128
TSTEPS = 1000
EPS = 1e-05
PATCH_ROWS = 256
BLOCKS = 64
IMAGES = 32
TEXTS = BLOCKS - IMAGES
STRIPES = 32
SROWS = 8
NZ = 8
WIDTH = 4096
LOCAL = WIDTH // NZ
S = BLOCKS * PATCH_ROWS
DOCS = 4
SEQ_AXES = ("x", "y", "c")
MASKED = -1e30
FLOOR = -1e29
SCALE2 = math.log2(math.e) / math.sqrt(HD)
QB = 16
KB = 16
TEXT_ROWS = TEXTS * SROWS
ROWS = BLOCKS * SROWS
VMEM = pl.BlockSpec(memory_space=pltpu.VMEM)
SMEM = pl.BlockSpec(memory_space=pltpu.SMEM)
ANY = pl.BlockSpec(memory_space=pl.ANY)
HBM = pl.BlockSpec(memory_space=pltpu.HBM)


def shifted(a, axis, shift):
    count = lax.axis_size(axis)
    return lax.ppermute(a, axis, [(i, (i + shift) % count) for i in range(count)])


def ring_pair(up, down):
    return shifted(up, "z", 1), shifted(down, "z", -1)


def ring_far(up, down):
    half = up.shape[0] // 2
    return shifted(up[:half], "z", 1), shifted(down[half:], "z", -1)


def nt_dot(a, b):
    return lax.dot_general(a, b, (((1,), (1,)), ((), ())), preferred_element_type=jnp.float32)


def pack_kernel(
    sc_ref, coef_ref, text_ref, clean_ref, noise_ref, feat_ref, wp_ref, wd_ref,
    out_ref, packed_ref,
):
    @pl.when(sc_ref[2] == 0)
    def _():
        packed_ref[...] = wp_ref[...]

    @pl.when(sc_ref[2] == 1)
    def _():
        packed_ref[...] = wd_ref[...]

    noise = noise_ref[...].astype(jnp.float32)
    noised = coef_ref[0] * clean_ref[...].astype(jnp.float32) + coef_ref[1] * noise
    pairs = jnp.transpose(jnp.concatenate([noised, noise], axis=0))
    feats = jnp.concatenate(
        [feat_ref[0:1, :HD], feat_ref[0:1, HD:], jnp.zeros((6, HD), jnp.float32)], axis=0
    )
    for s in range(0, STRIPES, 2):
        rows = [
            text_ref[b * PATCH_ROWS + s * SROWS : b * PATCH_ROWS + (s + 2) * SROWS, :].astype(
                jnp.float32
            )
            for b in range(2)
        ]
        for n in range(2):
            at = n * SROWS
            out_ref[s + n, :, :LOCAL] = jnp.concatenate(
                [rows[0][at : at + SROWS], rows[1][at : at + SROWS]], axis=0
            ).astype(jnp.bfloat16)
            patch = pairs[(s + n) * SROWS : (s + n + 1) * SROWS]
            out_ref[s + n, :, LOCAL:] = jnp.concatenate([patch, feats], axis=0).astype(jnp.bfloat16)


def sort_kernel(
    sc_ref, image_ref, doc_ref, got_ref, wt_ref,
    pay_ref, noised_ref, back_ref, times_ref, slot_ref, flag_ref, start_ref, text_ref, both_ref,
):
    seq = sc_ref[4]

    def clear(b, carry):
        flag_ref[b] = 0
        slot_ref[b] = 0
        return carry

    lax.fori_loop(0, BLOCKS, clear, 0)

    def mark(i, carry):
        block = image_ref[i]
        flag_ref[block] = 1
        slot_ref[block] = TEXTS + i
        return carry

    lax.fori_loop(0, IMAGES, mark, 0)
    docs = doc_ref[...]
    for d in range(DOCS):
        start_ref[d] = jnp.sum((docs < d).astype(jnp.int32))

    feats = jnp.concatenate(
        [got_ref[i, :, LOCAL:].astype(jnp.float32)[8:10].reshape(1, 2, HD) for i in range(IMAGES)],
        axis=0,
    )
    first, second = feats[:, 0, :].astype(jnp.bfloat16), feats[:, 1, :].astype(jnp.bfloat16)
    times = jnp.dot(first, wt_ref[:HD], preferred_element_type=jnp.float32) + jnp.dot(
        second, wt_ref[HD:], preferred_element_type=jnp.float32
    )
    both_ref[...] = times
    for n in range(2):
        image = jnp.maximum(slot_ref[2 * seq + n] - TEXTS, 0)
        times_ref[n : n + 1, :] = both_ref[pl.ds(image, 1), :]
    pay_ref[TEXT_ROWS:, :] = times.astype(jnp.bfloat16)

    def place(pair, rank):
        wide = got_ref[pair, :, :LOCAL].astype(jnp.float32)
        for n in range(2):
            b = 2 * pair + n
            is_text = flag_ref[b] == 0

            @pl.when(is_text)
            def _(b=b, n=n, rank=rank):
                slot_ref[b] = rank
                text_ref[pl.ds(pl.multiple_of(rank * SROWS, SROWS), SROWS), :] = wide[
                    n * SROWS : (n + 1) * SROWS
                ]

            rank = rank + jnp.where(is_text, 1, 0)
        return rank

    lax.fori_loop(0, BLOCKS // 2, place, 0)
    pay_ref[:TEXT_ROWS, :] = text_ref[...].astype(jnp.bfloat16)

    for i in range(0, IMAGES, 2):
        pair = jnp.concatenate(
            [got_ref[i + n, :, LOCAL:].astype(jnp.float32)[:SROWS] for n in range(2)], axis=0
        )
        noised_ref[i * SROWS : (i + 2) * SROWS, :] = pair[:, :64].astype(jnp.bfloat16)

    def back(pair, carry):
        parts = [
            got_ref[jnp.maximum(slot_ref[2 * pair + n] - TEXTS, 0), :, LOCAL:].astype(jnp.float32)[
                :SROWS
            ]
            for n in range(2)
        ]
        back_ref[pair] = jnp.concatenate(parts, axis=0).astype(jnp.bfloat16)
        return carry

    lax.fori_loop(0, BLOCKS // 2, back, 0)


def fold_chunks(
    z, shifts, chunks, w_hbm, wg_hbm, gain_ref, noised_ref, w_ref, wg_ref, sems,
    acc_ref, sq_ref, dec_ref,
):
    sources = [lax.rem(z - shift + NZ, NZ) for shift in shifts]
    copies = [
        (
            pltpu.make_async_copy(wg_hbm.at[:, src], wg_ref.at[n], sems.at[0, n]),
            pltpu.make_async_copy(w_hbm.at[:, src], w_ref.at[n], sems.at[1, n]),
        )
        for n, src in enumerate(sources)
    ]
    for pair in copies:
        pair[0].start()
        pair[1].start()
    for n, (src, block) in enumerate(zip(sources, chunks)):
        times = block[TEXT_ROWS:].astype(jnp.float32)
        copies[n][0].wait()
        patch = jnp.dot(noised_ref[...], wg_ref[n, 0], preferred_element_type=jnp.float32)
        timed = jnp.broadcast_to(times[:, None, :], (IMAGES, SROWS, LOCAL))
        image = (patch + timed.reshape(IMAGES * SROWS, LOCAL)).astype(jnp.bfloat16)
        both = jnp.concatenate([block[:TEXT_ROWS], image], axis=0)
        wide = both.astype(jnp.float32)
        square = wide * wide
        sq_ref[...] += sum(square[:, g * HD : (g + 1) * HD] for g in range(LOCAL // HD))
        dec_ref[...] += nt_dot(both, wg_ref[n, 1])
        left = (wide * gain_ref[src]).astype(jnp.bfloat16)
        copies[n][1].wait()
        for j in range(3):
            acc_ref[j] += jnp.dot(left, w_ref[n, j], preferred_element_type=jnp.float32)


def part_kernel(shifts, first, sc_ref, *refs):
    n = len(shifts)
    chunks, refs = refs[:n], refs[n:]
    w_hbm, wg_hbm, gain_ref, noised_ref = refs[:4]
    refs = refs[4:]
    moves = []
    if first:
        out_hbm, acc_ref, sq_ref, dec_ref, cut_hbm, w_ref, wg_ref, sems, cut_sems = refs
        rows = pl.ds(pl.multiple_of(sc_ref[2] * HD, HD), HD)
        for d in range(NZ):
            source = out_hbm.at[rows, d * LOCAL : (d + 1) * LOCAL]
            moves.append(pltpu.make_async_copy(source, cut_hbm.at[d], cut_sems.at[d]))
            moves[d].start()
        acc_ref[...] = jnp.zeros(acc_ref.shape, jnp.float32)
        sq_ref[...] = jnp.zeros(sq_ref.shape, jnp.float32)
        dec_ref[...] = jnp.zeros(dec_ref.shape, jnp.float32)
    else:
        acc_in, sq_in, dec_in, acc_ref, sq_ref, dec_ref, w_ref, wg_ref, sems = refs
        acc_ref[...] = acc_in[...]
        sq_ref[...] = sq_in[...]
        dec_ref[...] = dec_in[...]
    fold_chunks(
        sc_ref[3], shifts, [c[...] for c in chunks], w_hbm, wg_hbm, gain_ref, noised_ref,
        w_ref, wg_ref, sems, acc_ref, sq_ref, dec_ref,
    )
    for move in moves:
        move.wait()


def finish_kernel(
    sc_ref, slot_ref, f0, f1, w_hbm, wg_hbm, gain_ref, noised_ref, acc_in, sq_in, dec_in,
    my_q, my_kv, their_q, their_kv, dec_out,
    acc_ref, sq_ref, dec_ref, w_ref, wg_ref, sems, six_ref,
):
    c = sc_ref[2]
    acc_ref[...] = acc_in[...]
    sq_ref[...] = sq_in[...]
    dec_ref[...] = dec_in[...]
    fold_chunks(
        sc_ref[3], (4,), [jnp.concatenate([f0[...], f1[...]], axis=0)], w_hbm, wg_hbm, gain_ref, noised_ref,
        w_ref, wg_ref, sems, acc_ref, sq_ref, dec_ref,
    )
    squares = jnp.sum(sq_ref[...], axis=1, keepdims=True)
    inverse = lax.rsqrt(squares * (1.0 / WIDTH) + EPS)
    for j in range(3):
        scale = inverse * SCALE2 if j == 0 else inverse
        for h in range(2):
            six_ref[2 * j + h] = acc_ref[j, :, h * HD : (h + 1) * HD] * scale

    def arrange(pair, carry):
        first = pl.multiple_of(slot_ref[2 * pair] * SROWS, SROWS)
        second = pl.multiple_of(slot_ref[2 * pair + 1] * SROWS, SROWS)
        at = pl.ds(pl.multiple_of(pair * 2 * SROWS, 2 * SROWS), 2 * SROWS)

        def rows_of(index):
            return jnp.concatenate(
                [six_ref[index, pl.ds(first, SROWS), :], six_ref[index, pl.ds(second, SROWS), :]],
                axis=0,
            ).astype(jnp.bfloat16)

        for q_ref, kv_ref, head in ((my_q, my_kv, c), (their_q, their_kv, 1 - c)):
            q_ref[at, :] = rows_of(head)
            kv_ref[0, at, :] = rows_of(2 + head)
            kv_ref[1, at, :] = rows_of(4 + head)
        dec_out[pair] = jnp.concatenate(
            [dec_ref[pl.ds(first, SROWS), :], dec_ref[pl.ds(second, SROWS), :]], axis=1
        )
        return carry

    lax.fori_loop(0, BLOCKS // 2, arrange, 0)


def attend_kernel(
    sc_ref, start_ref, flag_ref, q0, q1, q2, q3, kv0, kv1, kv3, k2, v2, dec_ref, img_ref,
    out_ref, qs, ks, vs, vx, m_ref, acc_ref, low_ref, high_ref, s_even, s_odd, t_even, t_odd, sems,
):
    x, y, c = sc_ref[0], sc_ref[1], sc_ref[2]
    copies = []

    def bring(source, target):
        copy = pltpu.make_async_copy(source, target, sems.at[len(copies)])
        copy.start()
        copies.append(copy)

    for i in range(2):
        cc = c if i == 0 else 1 - c
        for ref, shift in ((kv0, 0), (kv1, 1), (kv3, 3)):
            at = lax.rem(x - shift + 4, 4) * 2 + cc
            bring(ref.at[i, 1], vs.at[:, at])
            bring(ref.at[i, 0], ks.at[:, at])
        at = lax.rem(x + 2, 4) * 2 + cc
        bring(v2.at[i], vs.at[:, at])
        bring(k2.at[i], ks.at[:, at])
        for ref, shift in ((q0, 0), (q1, 1), (q2, 2), (q3, 3)):
            bring(ref.at[i], qs.at[:, lax.rem(y - shift + 4, 4) * 2 + cc])

    rows = QB * 64
    cols = KB * 64
    half = cols // 2
    span = QB * PATCH_ROWS
    dests = QB // 2
    tiles = BLOCKS // QB
    starts = [start_ref[d] for d in range(DOCS)]
    for i in range(tiles):
        rho = lax.broadcasted_iota(jnp.int32, (8, rows), 1)
        blk = 2 * (rho >> 7) + ((rho >> 3) & 1)
        first = (QB * i + blk) * PATCH_ROWS
        q_pos = first + 64 * x + 8 * ((rho >> 4) & 7) + (rho & 7)
        low = jnp.zeros((8, rows), jnp.int32)
        high_doc = jnp.full((8, rows), S - 1, jnp.int32)
        for start in starts:
            low = jnp.where(start <= q_pos, jnp.maximum(low, start), low)
            high_doc = jnp.where(start > q_pos, jnp.minimum(high_doc, start - 1), high_doc)
        flag = jnp.zeros((8, rows), jnp.int32)
        for n in range(QB):
            flag = jnp.where(blk == n, flag_ref[QB * i + n], flag)
        low_ref[i] = low
        high_ref[i] = jnp.where(flag == 1, jnp.minimum(high_doc, first + PATCH_ROWS - 1), q_pos)
    acc_ref[...] = jnp.zeros((HD + 16, rows), jnp.float32)
    m_ref[...] = jnp.zeros((8, rows), jnp.float32)
    for copy in copies:
        copy.wait()
    for h in range(2 * tiles):
        values = vs[h].reshape(half, HD).astype(jnp.float32)
        vx[h, :HD, :] = jnp.transpose(values).astype(jnp.bfloat16)
        vx[h, HD:, :] = jnp.ones((16, half), jnp.bfloat16)

    score_refs, top_refs = (s_even, s_odd), (t_even, t_odd)
    count = tiles * (tiles + 1) // 2

    def tile_of(t):
        i = sum((t >= n * (n + 1) // 2).astype(jnp.int32) for n in range(1, tiles))
        return i, t - (i * (i + 1)) // 2

    def score(t, slot, kind):
        i, j = tile_of(t)
        score_ref, top_ref = score_refs[slot], top_refs[slot]
        k = ks[pl.ds(2 * j, 2)].reshape(cols, HD)
        q = qs[pl.ds(i * dests, dests)].reshape(rows, HD)

        def masked(s, first_key, lanes):
            kappa = lax.broadcasted_iota(jnp.int32, (s.shape[0], 1), 0) + first_key
            k_pos = (
                (KB * j + 8 * (kappa >> 9) + ((kappa >> 3) & 7)) * PATCH_ROWS
                + 64 * ((kappa >> 7) & 3) + 16 * y + 8 * ((kappa >> 6) & 1) + (kappa & 7)
            )
            seen = jnp.logical_and(k_pos >= low_ref[i, 0:1, lanes], k_pos <= high_ref[i, 0:1, lanes])
            return jnp.where(seen, s, MASKED)

        if kind == "diagonal":
            s = masked(nt_dot(k[:half], q), 0, slice(0, rows))
            late = masked(nt_dot(k[half:], q[half:]), half, slice(half, rows))
            score_ref[:half, :] = s
            score_ref[half:, half:] = late
            top = jnp.max(s, axis=0, keepdims=True)
            top_ref[0:1, :half] = top[:, :half]
            top_ref[0:1, half:] = jnp.maximum(top[:, half:], jnp.max(late, axis=0, keepdims=True))
        else:
            s = nt_dot(k, q)
            if kind == "masked":
                s = masked(s, 0, slice(0, rows))
            score_ref[...] = s
            top_ref[0:1] = jnp.max(s, axis=0, keepdims=True)

    def weigh(t, slot, diagonal):
        i, j = tile_of(t)
        score_ref = score_refs[slot]
        m_old = jnp.where(j == 0, FLOOR, m_ref[0:1])
        m_new = jnp.maximum(m_old, top_refs[slot][0:1])
        m_ref[0:1] = m_new
        alpha = jnp.where(j == 0, 0.0, jnp.exp2(m_old - m_new))
        if diagonal:
            p = jnp.exp2(score_ref[:half, :] - m_new).astype(jnp.bfloat16)
            late = jnp.exp2(score_ref[half:, half:] - m_new[:, half:]).astype(jnp.bfloat16)
            acc_ref[...] = acc_ref[...] * alpha + jnp.dot(
                vx[2 * j], p, preferred_element_type=jnp.float32
            )
            acc_ref[:, half:] += jnp.dot(vx[2 * j + 1], late, preferred_element_type=jnp.float32)
        else:
            p = jnp.exp2(score_ref[...] - m_new).astype(jnp.bfloat16)
            v = jnp.concatenate([vx[2 * j], vx[2 * j + 1]], axis=1)
            acc_ref[...] = acc_ref[...] * alpha + jnp.dot(v, p, preferred_element_type=jnp.float32)

    def emit(t):
        i, j = tile_of(t)

        @pl.when(i == j)
        def _():
            total = acc_ref[HD : HD + 1]
            some = total > 0.0
            safe = jnp.where(some, total, 1.0)
            o = jnp.transpose(acc_ref[:HD] / safe).astype(jnp.bfloat16)
            level = jnp.where(some, m_ref[0:1] + jnp.log2(safe), MASKED)
            high_part = level.astype(jnp.bfloat16).astype(jnp.float32)
            rest = level - high_part
            mid_part = rest.astype(jnp.bfloat16).astype(jnp.float32)
            low_part = rest - mid_part
            head = jnp.concatenate(
                [high_part, mid_part, low_part, jnp.zeros((5, rows), jnp.float32)], axis=0
            )
            for d in range(dests):
                dest = dests * i + d
                out_ref[dest, 0:8] = o[HD * d : HD * (d + 1)].reshape(8, 16, HD)
                out_ref[dest, 8] = jnp.concatenate(
                    [head[:, HD * d : HD * (d + 1)], dec_ref[dest]], axis=0
                ).astype(jnp.bfloat16)
                out_ref[dest, 9] = img_ref[dest]

    def advance(t, slot):
        i, j = tile_of(t + 1)
        last = i * span + span - 1
        low_last = 0
        for start in starts:
            low_last = jnp.where(start <= last, jnp.maximum(start, low_last), low_last)
        i_now, j_now = tile_of(t)
        on_diagonal = i_now == j_now
        full = jnp.logical_and(j < i, low_last <= j * span)

        @pl.when(on_diagonal)
        def _():
            score(t + 1, 1 - slot, "masked")
            weigh(t, slot, True)

        @pl.when(jnp.logical_and(jnp.logical_not(on_diagonal), full))
        def _():
            score(t + 1, 1 - slot, "full")
            weigh(t, slot, False)

        @pl.when(jnp.logical_and(jnp.logical_not(on_diagonal), i == j))
        def _():
            score(t + 1, 1 - slot, "diagonal")
            weigh(t, slot, False)

        @pl.when(jnp.logical_not(on_diagonal | full | (i == j)))
        def _():
            score(t + 1, 1 - slot, "masked")
            weigh(t, slot, False)

        emit(t)

    def two(u, carry):
        advance(2 * u, 0)
        advance(2 * u + 1, 1)
        return carry

    score(jnp.int32(0), 0, "diagonal")
    lax.fori_loop(0, (count - 2) // 2, two, 0)
    advance(jnp.int32(count - 2), 0)
    weigh(jnp.int32(count - 1), 1, True)
    emit(jnp.int32(count - 1))


def combine_kernel(in_ref, w2_ref, att_ref, dec_ref, full_ref):
    for x in range(4):
        for c in range(2):
            heads = [in_ref[x * 8 + y * 2 + c, 8].astype(jnp.float32) for y in range(4)]
            levels = [h[0:1] + h[1:2] + h[2:3] for h in heads]
            top = functools.reduce(jnp.maximum, levels)
            weights = [jnp.exp2(level - top) for level in levels]
            total = functools.reduce(jnp.add, weights)
            part = None
            for y in range(4):
                share = jnp.transpose(jnp.broadcast_to(weights[y] / total, (HD, HD)))
                o = in_ref[x * 8 + y * 2 + c, 0:8].reshape(HD, HD).astype(jnp.float32)
                part = o * share if part is None else part + o * share
            for p in range(8):
                for b in range(2):
                    full_ref[
                        b * PATCH_ROWS + 64 * x + 8 * p : b * PATCH_ROWS + 64 * x + 8 * p + 8,
                        c * HD : (c + 1) * HD,
                    ] = part[(2 * p + b) * 8 : (2 * p + b) * 8 + 8]
            for y in range(4):
                stripe = x * 8 + y * 2 + c
                for b in range(2):
                    at = b * PATCH_ROWS + stripe * SROWS
                    dec_ref[at : at + SROWS, :] = heads[y][8:16, b * 64 : (b + 1) * 64]
    att_ref[:ROWS, :] = full_ref[...].astype(jnp.bfloat16)
    att_ref[ROWS:, :] = w2_ref[...]


def project_chunks(sc_ref, shifts, chunks, mine_hbm, theirs_hbm, cols_ref, sems, hid_ref, pred_ref):
    c, z = sc_ref[2], sc_ref[3]
    copies = []
    for n, shift in enumerate(shifts):
        src = lax.rem(z - shift + NZ, NZ)
        for m, (hbm, half) in enumerate(((mine_hbm, c), (theirs_hbm, 1 - c))):
            rows = pl.ds(pl.multiple_of(half * HD, HD), HD)
            copies.append(
                pltpu.make_async_copy(hbm.at[src], cols_ref.at[n, rows], sems.at[m, n])
            )
            copies[-1].start()
    for n, block in enumerate(chunks):
        attended = block[:ROWS]
        pred_ref[...] += nt_dot(attended, block[ROWS:])
        copies[2 * n].wait()
        copies[2 * n + 1].wait()
        hid_ref[...] += jnp.dot(attended, cols_ref[n], preferred_element_type=jnp.float32)


def start_kernel(
    sc_ref, flag_ref, c0, c1, c2, mine_hbm, theirs_hbm, parts_ref, text_ref, wp_ref, times_ref, dec_ref,
    hid_ref, pred_ref, noise_ref, cols_ref, sems,
):
    seq = sc_ref[4]
    for b in range(2):
        at = slice(b * PATCH_ROWS, (b + 1) * PATCH_ROWS)
        pairs = parts_ref[...].astype(jnp.float32)[:, b * SROWS : (b + 1) * SROWS].reshape(
            PATCH_ROWS, 2 * 64
        )
        noise_ref[at, :] = pairs[:, 64:]
        patch = jnp.dot(
            pairs[:, :64].astype(jnp.bfloat16), wp_ref[...], preferred_element_type=jnp.float32
        )
        image = (patch + times_ref[b : b + 1, :]).astype(jnp.bfloat16).astype(jnp.float32)
        text = text_ref[at, :].astype(jnp.float32)
        hid_ref[at, :] = jnp.where(flag_ref[2 * seq + b] == 1, image, text)
    pred_ref[...] = dec_ref[...]
    project_chunks(
        sc_ref, (0, 1, -1), [c0[...], c1[...], c2[...]], mine_hbm, theirs_hbm, cols_ref, sems,
        hid_ref, pred_ref,
    )


def middle_kernel(
    shifts, sc_ref, c0, c1, mine_hbm, theirs_hbm, hid_in, pred_in, hid_ref, pred_ref, cols_ref, sems
):
    hid_ref[...] = hid_in[...]
    pred_ref[...] = pred_in[...]
    project_chunks(
        sc_ref, shifts, [c0[...], c1[...]], mine_hbm, theirs_hbm, cols_ref, sems,
        hid_ref, pred_ref,
    )


def close_kernel(
    sc_ref, flag_ref, f0, f1, mine_hbm, theirs_hbm, hid_in, pred_in, noise_ref,
    out_ref, pred_t_ref, err_ref, hid_ref, pred_ref, cols_ref, sems,
):
    seq = sc_ref[4]
    hid_ref[...] = hid_in[...]
    pred_ref[...] = pred_in[...]
    project_chunks(
        sc_ref, (4,), [jnp.concatenate([f0[...], f1[...]], axis=0)], mine_hbm, theirs_hbm, cols_ref, sems, hid_ref, pred_ref
    )
    out_ref[...] = hid_ref[...].astype(jnp.bfloat16)
    pred_t_ref[...] = jnp.transpose(pred_ref[...])
    gap = pred_ref[...] - noise_ref[...]
    square = jnp.transpose(gap * gap)
    mean = jnp.sum(square, axis=0, keepdims=True) * (1.0 / 64)
    for b in range(2):
        at = slice(b * PATCH_ROWS, (b + 1) * PATCH_ROWS)
        err_ref[0:1, at] = jnp.where(flag_ref[2 * seq + b] == 1, mean[:, at], 0.0)


def kernel_params(mib):
    return pltpu.CompilerParams(vmem_limit_bytes=mib * 1024 * 1024)


def call(kernel, name, outs, in_specs, args, scratch=(), mib=24, flops=0, nbytes=0, out_specs=None):
    return pl.pallas_call(
        kernel,
        out_shape=tuple(jax.ShapeDtypeStruct(shape, dtype) for shape, dtype in outs),
        in_specs=in_specs,
        out_specs=out_specs or tuple(VMEM for _ in outs),
        scratch_shapes=list(scratch),
        compiler_params=kernel_params(mib),
        cost_estimate=pl.CostEstimate(flops=flops, bytes_accessed=nbytes, transcendentals=0),
        name=name,
    )(*args)


def per_device(
    text_embed, latents, noise, timesteps, image_block, doc_ids, norm_gain,
    w_patch, w_time, w_qkv, w_out, w_dec,
):
    ix, iy, ic, iz = (lax.axis_index(a) for a in ("x", "y", "c", "z"))
    seq = ix * 8 + iy * 2 + ic
    f32, bf16, i32 = jnp.float32, jnp.bfloat16, jnp.int32
    scalars = jnp.stack([ix, iy, ic, iz, seq]).astype(i32)

    step = timesteps.astype(f32)
    signal = jnp.cos((step / TSTEPS + 0.008) / 1.008 * (math.pi / 2)) ** 2
    coefs = jnp.concatenate([jnp.sqrt(signal), jnp.sqrt(1.0 - signal)])
    freq_count = w_time.shape[0] // 2
    freqs = jnp.exp(-math.log(10000.0) * jnp.arange(freq_count, dtype=f32) / freq_count)
    angles = step[:, None] * freqs[None, :]
    feats = jnp.concatenate([jnp.cos(angles), jnp.sin(angles)], axis=1)
    sent, packed = call(
        pack_kernel, "pack",
        [((STRIPES, 2 * SROWS, LOCAL + HD), bf16), ((64, LOCAL), bf16)], [SMEM] * 2 + [VMEM] * 6,
        (scalars, coefs, text_embed, latents[0].T, noise[0].T, feats, w_patch, w_dec.T), mib=60,
    )
    got = lax.all_to_all(sent, SEQ_AXES, 0, 0, tiled=False)
    wg = lax.all_gather(packed, ("c", "z"), axis=0, tiled=False).reshape(2, NZ, 64, LOCAL)

    payload, noised, image_back, own_times, slots, flags, starts = call(
        sort_kernel, "sort",
        [
            ((TEXT_ROWS + IMAGES, LOCAL), bf16),
            ((IMAGES * SROWS, 64), bf16),
            ((STRIPES, 2 * SROWS, HD), bf16),
            ((2, LOCAL), f32),
            ((BLOCKS,), i32),
            ((BLOCKS,), i32),
            ((DOCS,), i32),
        ],
        [SMEM, SMEM, VMEM, VMEM, VMEM],
        (scalars, image_block, doc_ids.reshape(128, 128), got, w_time),
        scratch=[pltpu.VMEM((TEXT_ROWS, LOCAL), f32), pltpu.VMEM((IMAGES, LOCAL), f32)],
        mib=16, out_specs=(VMEM,) * 4 + (SMEM,) * 3,
    )
    w_cols = w_qkv.transpose(1, 0, 2).reshape(3, NZ, LOCAL, 2 * HD)
    gains = norm_gain.reshape(NZ, 1, LOCAL)
    sums = [((3, ROWS, 2 * HD), f32), ((ROWS, HD), f32), ((ROWS, 64), f32)]

    def fold(shifts, chunks, state):
        count = len(shifts)
        scratch = [
            pltpu.VMEM((count, 3, LOCAL, 2 * HD), bf16),
            pltpu.VMEM((count, 2, 64, LOCAL), bf16),
            pltpu.SemaphoreType.DMA((2, count)),
        ]
        cost = {"flops": count * 2 * ROWS * LOCAL * 6 * HD, "nbytes": 4 << 20}
        kernel = functools.partial(part_kernel, shifts, not state)
        specs = [SMEM] + [VMEM] * count + [HBM] * 2 + [VMEM] * 2
        given = (scalars, *chunks, w_cols, wg, gains, noised)
        if state:
            return call(
                kernel, "part", sums, specs + [VMEM] * 3, (*given, *state), scratch=scratch, **cost
            )
        return call(
            kernel, "part", sums + [((NZ, HD, LOCAL), bf16)], specs + [HBM], (*given, w_out),
            scratch=scratch + [pltpu.SemaphoreType.DMA((NZ,))],
            **cost,
        )

    up1, down1 = ring_pair(payload, payload)
    up2, down2 = ring_pair(up1, down1)
    *state, out_rows = fold((0, 1, -1), (payload, up1, down1), ())
    up2, down2, *state = lax.optimization_barrier((up2, down2, *state))
    up3, down3 = ring_pair(up2, down2)
    state = fold((2, -2), (up2, down2), state)
    up3, down3, out_rows, *state = lax.optimization_barrier((up3, down3, out_rows, *state))
    far = ring_far(up3, down3)
    cols_mine = lax.all_to_all(out_rows, "z", 0, 0, tiled=False)
    state = fold((3, -3), (up3, down3), state)
    my_q, my_kv, their_q, their_kv, dec_rows = call(
        finish_kernel, "finish",
        [
            ((ROWS, HD), bf16),
            ((2, ROWS, HD), bf16),
            ((ROWS, HD), bf16),
            ((2, ROWS, HD), bf16),
            ((STRIPES, SROWS, HD), f32),
        ],
        [SMEM, SMEM, VMEM, VMEM, HBM, HBM] + [VMEM] * 5,
        (scalars, slots, *far, w_cols, wg, gains, noised, *state),
        scratch=[
            pltpu.VMEM((3, ROWS, 2 * HD), f32),
            pltpu.VMEM((ROWS, HD), f32),
            pltpu.VMEM((ROWS, 64), f32),
            pltpu.VMEM((1, 3, LOCAL, 2 * HD), bf16),
            pltpu.VMEM((1, 2, 64, LOCAL), bf16),
            pltpu.SemaphoreType.DMA((2, 1)),
            pltpu.VMEM((6, ROWS, HD), f32),
        ],
    )

    got_q = lax.ppermute(their_q, "c", [(0, 1), (1, 0)])
    got_kv = lax.ppermute(their_kv, "c", [(0, 1), (1, 0)])
    q = jnp.stack([my_q, got_q])
    kv = jnp.stack([my_kv, got_kv])
    kv1, kv3 = shifted(kv, "x", 1), shifted(kv, "x", -1)
    q1, q3 = shifted(q, "y", 1), shifted(q, "y", -1)
    k2, v2 = shifted(kv1[:, 0], "x", 1), shifted(kv3[:, 1], "x", -1)
    q2 = shifted(q, "y", 2)
    keyed = [a.reshape(2, 2, 8, 64, HD) for a in (kv, kv1, kv3)]
    keyed += [a.reshape(2, 8, 64, HD) for a in (k2, v2)]
    by_dest = [a.reshape(2, STRIPES, 16, HD) for a in (q, q1, q2, q3)]

    (partial,) = call(
        attend_kernel, "attend", [((STRIPES, 10, 16, HD), bf16)],
        [SMEM] * 3 + [ANY] * 9 + [VMEM] * 2,
        (scalars, starts, flags, *by_dest, *keyed, dec_rows, image_back),
        scratch=[
            pltpu.VMEM((STRIPES, 8, 16, HD), bf16),
            pltpu.VMEM((8, 8, 64, HD), bf16),
            pltpu.VMEM((8, 8, 64, HD), bf16),
            pltpu.VMEM((8, HD + 16, ROWS), bf16),
            pltpu.VMEM((8, QB * 64), f32),
            pltpu.VMEM((HD + 16, QB * 64), f32),
            pltpu.VMEM((BLOCKS // QB, 8, QB * 64), i32),
            pltpu.VMEM((BLOCKS // QB, 8, QB * 64), i32),
            pltpu.VMEM((KB * 64, QB * 64), f32),
            pltpu.VMEM((KB * 64, QB * 64), f32),
            pltpu.VMEM((8, QB * 64), f32),
            pltpu.VMEM((8, QB * 64), f32),
            pltpu.SemaphoreType.DMA((24,)),
        ],
        mib=32, flops=5 << 30, nbytes=8 << 20,
    )
    partial, cols_mine = lax.optimization_barrier((partial, cols_mine))
    cols_theirs = lax.ppermute(cols_mine, "c", [(0, 1), (1, 0)])
    parts = lax.all_to_all(partial, SEQ_AXES, 0, 0, tiled=False)

    w_dec_t = wg[1].transpose(1, 0, 2).reshape(64, WIDTH)
    w2_t = nt_dot(w_dec_t, w_out).astype(bf16)

    att, dec_own = call(
        combine_kernel, "combine",
        [((ROWS + 64, 2 * HD), bf16), ((ROWS, 64), f32)], [VMEM, VMEM], (parts, w2_t),
        scratch=[pltpu.VMEM((ROWS, 2 * HD), f32)],
    )
    hid_out = [((ROWS, LOCAL), f32), ((ROWS, 64), f32)]

    def cols_scratch(count):
        return [
            pltpu.VMEM((count, 2 * HD, LOCAL), bf16), pltpu.SemaphoreType.DMA((2, count)),
        ]

    def project(shifts, chunks, hid, pred):
        return call(
            functools.partial(middle_kernel, shifts), "middle", hid_out,
            [SMEM] + [VMEM] * 2 + [ANY] * 2 + [VMEM] * 2,
            (scalars, *chunks, cols_mine, cols_theirs, hid, pred),
            scratch=cols_scratch(2), flops=2 * 2 * ROWS * 256 * LOCAL, nbytes=4 << 20,
        )

    up1, down1 = ring_pair(att, att)
    up2, down2 = ring_pair(up1, down1)
    hid, pred, own_noise = call(
        start_kernel, "start", hid_out + [((ROWS, 64), f32)],
        [SMEM, SMEM] + [VMEM] * 3 + [ANY] * 2 + [VMEM] * 5,
        (
            scalars, flags, att, up1, down1, cols_mine, cols_theirs, parts[:, 9], text_embed, w_patch,
            own_times, dec_own,
        ),
        scratch=cols_scratch(3), flops=3 * 2 * ROWS * 256 * LOCAL, nbytes=4 << 20,
    )
    up2, down2, hid, pred = lax.optimization_barrier((up2, down2, hid, pred))
    up3, down3 = ring_pair(up2, down2)
    hid, pred = project((2, -2), (up2, down2), hid, pred)
    up3, down3, hid, pred = lax.optimization_barrier((up3, down3, hid, pred))
    far = ring_far(up3, down3)
    hid, pred = project((3, -3), (up3, down3), hid, pred)
    hidden_out, predicted_t, error = call(
        close_kernel, "close",
        [((ROWS, LOCAL), bf16), ((64, ROWS), f32), ((1, ROWS), f32)],
        [SMEM, SMEM] + [VMEM] * 2 + [ANY] * 2 + [VMEM] * 3,
        (scalars, flags, *far, cols_mine, cols_theirs, hid, pred, own_noise),
        scratch=[pltpu.VMEM((ROWS, LOCAL), f32), pltpu.VMEM((ROWS, 64), f32)] + cols_scratch(1),
    )
    return hidden_out, predicted_t.T, error.reshape(ROWS)


def solution(mesh):
    fine = Mesh(mesh.devices.reshape(4, 4, 2, NZ), ("x", "y", "c", "z"))
    seq, tp = SEQ_AXES, "z"
    in_specs = (
        P(seq, tp),
        P(seq, None, None),
        P(seq, None, None),
        P(seq),
        P(),
        P(),
        P(),
        P(None, tp),
        P(None, tp),
        P(None, None, tp),
        P(tp, None),
        P(tp, None),
    )
    out_specs = (P(seq, tp), P(seq, None), P(seq))
    return jax.shard_map(
        per_device, mesh=fine, in_specs=in_specs, out_specs=out_specs, check_vma=False
    )
```
